32 devices in a mesh: parts: 2 (over x), tile: 8 (over z, y), chan: 2 (over core).
Axes of the slice: x: 2, y: 2, z: 4, core: 2. Of those that a mesh axis runs over, the one named last changes fastest.
Arguments:
- activations: bfloat16 [384, 16, 16, 128], P(('parts', 'tile')), parts along dimension 0, may hold values from -6 to 6
- cotangent: bfloat16 [384, 16, 16, 128], P(('parts', 'tile')), parts along dimension 0, may hold values from -6 to 6
- neighbours: int32 [192, 4], P('tile'), may hold values from 0 to 191, as said below
- rotations: int32 [192, 4], P('tile'), may hold values from 0 to 3, as said below
- kernels: bfloat16 [2, 7, 7, 128], replicated, may hold values from -0.875 to 0.875
- gains: float32 [2, 128], replicated, may hold values from 0.1 to 1.9
- w_in: bfloat16 [2, 128, 512], P(None, None, 'chan'), may hold values from -0.5 to 0.5
- w_out: bfloat16 [2, 512, 128], P(None, 'chan'), may hold values from -0.25 to 0.25
Outputs:
- input_grads: bfloat16 [384, 16, 16, 128], P(('parts', 'tile')), parts along dimension 0
- kernel_grads: float32 [4, 7, 7, 128], P('parts'), parts along dimension 0
- gain_grads: float32 [4, 128], P('parts'), parts along dimension 0
- w_in_grads: float32 [4, 128, 512], P('parts', None, 'chan'), parts along dimension 0
- w_out_grads: float32 [4, 512, 128], P('parts', 'chan'), parts along dimension 0
The draws below stay inside these ranges and needn't reach their ends.
There are 2 independent parts, one for each index of `parts`. The reference program is written for one: setup_inputs(seed, part) draws one part's arguments, and reference() takes and returns one part's arrays. A program takes and returns all parts, laid end to end along the dimension named above; an argument that names none is the same for every part. Nothing has to cross between parts.
Inputs may be any that keep to these rules, and one draw needn't show every extreme that they name: `neighbours`: tile g lies in block g // 24; the tile across any side of a tile lies in the same block or in the block just before or after it (cyclically, 8 blocks); adjacency is mutual. The rotations of the two sides of a seam add up to 0 mod 4.
All inputs are finite; a program needn't handle non-finite values.
Results may differ from the reference program's by a relative error of at most 0.02.
Values may be sent and summed in bfloat16 or wider, within the bound.
A program may use at most 384 MiB of HBM per device.

```python
import jax
import jax.numpy as jnp
from jax import lax

C = 128
F = 512
KS = 7
BLOCKS = 2
TILES = 192
S = 16
TILE_DEV = 24
N_CHAN = 2


def tile_layout(key):
    cycle_rows = TILE_DEV
    cycle_columns = TILES // TILE_DEV
    column_keys = jax.random.split(jax.random.fold_in(key, 101), cycle_columns)
    orders = jax.vmap(lambda column_key: jax.random.permutation(column_key, cycle_rows))(column_keys).astype(jnp.int32)
    quarters = jax.random.randint(jax.random.fold_in(key, 102), (TILES,), 0, 4, dtype=jnp.int32)
    column_ids = jnp.arange(cycle_columns, dtype=jnp.int32)[:, None]
    row_ids = jnp.arange(cycle_rows, dtype=jnp.int32)[None, :]
    labels = column_ids * cycle_rows + orders

    def located(column_step, row_step):
        return labels[(column_ids + column_step) % cycle_columns, (row_ids + row_step) % cycle_rows]
    true_sides = jnp.stack([located(0, -1), located(1, 0), located(0, 1), located(-1, 0)], -1).reshape(TILES, 4)
    position = jnp.zeros((TILES,), jnp.int32).at[labels.reshape(-1)].set(jnp.arange(TILES, dtype=jnp.int32))
    by_tile = true_sides[position]
    stored = (jnp.arange(4, dtype=jnp.int32)[None, :] + quarters[:, None]) % 4
    neighbours = jnp.take_along_axis(by_tile, stored, 1)
    rotations = (quarters[:, None] - quarters[neighbours]) % 4
    return (neighbours.astype(jnp.int32), rotations.astype(jnp.int32))


def draw_neighbours(key, part):
    neighbours, rotations = tile_layout(key)
    return neighbours


def draw_rotations(key, part):
    neighbours, rotations = tile_layout(key)
    return rotations


def levels(stream_key, extent, cuts, least, largest):
    def one(dim, parts):
        steps = jax.random.uniform(jax.random.fold_in(jax.random.fold_in(stream_key, 6), dim), (parts,), jnp.float32, least / len(cuts), largest / len(cuts))
        return jnp.repeat(jnp.exp(steps), extent[dim] // parts).reshape((-1,) + (1,) * (len(extent) - dim - 1))

    level = one(*cuts[0])
    for cut in cuts[1:]:
        level = level * one(*cut)
    return level


def scatter_about(key, extent, scale, most, pieces=(), kind=jnp.bfloat16):
    entries = jax.random.normal(key, extent, jnp.float32) * scale
    if len(pieces) > 0:
        entries = levels(key, extent, pieces, -0.22, 0.18) * entries
    return jnp.clip(entries, min=-most, max=most).astype(kind)


def setup_inputs(seed: int = 0, part: int = 0) -> dict:
    seeds = jax.random.split(jax.random.key(seed), 9)
    own_keys = jax.random.split(jax.random.fold_in(seeds[8], part), 9)
    activations = scatter_about(own_keys[0], (TILES, S, S, C), 1.0, 6.0, ((0, 8),))
    cotangent = scatter_about(own_keys[1], (TILES, S, S, C), 1.0, 6.0, ((0, 8),))
    neighbours = draw_neighbours(jax.random.fold_in(seeds[8], 71), part)
    rotations = draw_rotations(jax.random.fold_in(seeds[8], 71), part)
    kernels = scatter_about(seeds[4], (BLOCKS, KS, KS, C), (KS * KS) ** -0.5, 0.875)
    gains = jnp.clip(1.0 + 0.18 * jax.random.normal(seeds[5], (BLOCKS, C), jnp.float32), 0.1, 1.9)
    w_in = scatter_about(seeds[6], (BLOCKS, C, F), C ** -0.5, 0.5, ((2, 2),))
    w_out = scatter_about(seeds[7], (BLOCKS, F, C), F ** -0.5, 0.25, ((1, 2),))
    return {"activations": activations, "cotangent": cotangent, "neighbours": neighbours, "rotations": rotations, "kernels": kernels, "gains": gains, "w_in": w_in, "w_out": w_out}


def edge_strips(tile_data, pad_depth):
    return jnp.stack([jnp.rot90(tile_data, quarter, axes=(1, 2))[:, :pad_depth] for quarter in range(4)], 1)

def side_sources(rotations):
    return (jnp.arange(4, dtype=jnp.int32)[None, :] + 2 + rotations) % 4

def assemble(tile_data, chosen, pad_depth):
    regions = [jnp.rot90(chosen[:, side_index], -((side_index + 2) % 4), axes=(1, 2)) for side_index in range(4)]
    corner = jnp.zeros((tile_data.shape[0], pad_depth, pad_depth, tile_data.shape[3]), tile_data.dtype)
    middle = jnp.concatenate([regions[3], tile_data, regions[1]], 2)
    upper_rows = jnp.concatenate([corner, regions[0], corner], 2)
    lower_rows = jnp.concatenate([corner, regions[2], corner], 2)
    return jnp.concatenate([upper_rows, middle, lower_rows], 1)

def pad_tiles(tile_data, neighbours, rotations, pad_depth):
    strips = edge_strips(tile_data, pad_depth)
    chosen = strips[neighbours, side_sources(rotations)]
    return assemble(tile_data, chosen, pad_depth)

def depthwise(padded, kernel):
    kernel_size = kernel.shape[0]
    out_side = padded.shape[1] - kernel_size + 1
    running = jnp.zeros((padded.shape[0], out_side, out_side, padded.shape[3]), jnp.float32)
    for kernel_row in range(kernel_size):
        for kernel_column in range(kernel_size):
            window = padded[:, kernel_row:kernel_row + out_side, kernel_column:kernel_column + out_side]
            running = running + window.astype(jnp.float32) * kernel[kernel_row, kernel_column].astype(jnp.float32)
    return running

def depthwise_back(padded, grad_hidden, kernel):
    kernel_size = kernel.shape[0]
    out_side = grad_hidden.shape[1]
    grad_padded = jnp.zeros(padded.shape, jnp.float32)
    rows_grad = []
    for kernel_row in range(kernel_size):
        column_grad = []
        for kernel_column in range(kernel_size):
            window = padded[:, kernel_row:kernel_row + out_side, kernel_column:kernel_column + out_side]
            column_grad.append(lax.optimization_barrier(jnp.sum(window.astype(jnp.float32) * grad_hidden, axis=(0, 1, 2))))
            spread = grad_hidden * kernel[kernel_row, kernel_column].astype(jnp.float32)
            grad_padded = grad_padded + jnp.pad(spread, ((0, 0), (kernel_row, kernel_size - 1 - kernel_row), (kernel_column, kernel_size - 1 - kernel_column), (0, 0)))
        rows_grad.append(jnp.stack(column_grad))
    return (jnp.stack(rows_grad), grad_padded)

def side_canon(grad_padded, pad_depth):
    tile_side = grad_padded.shape[1] - 2 * pad_depth
    inner_end = pad_depth + tile_side
    regions = [grad_padded[:, :pad_depth, pad_depth:inner_end], grad_padded[:, pad_depth:inner_end, inner_end:], grad_padded[:, inner_end:, pad_depth:inner_end], grad_padded[:, pad_depth:inner_end, :pad_depth]]
    canon = jnp.stack([jnp.rot90(regions[side_index], (side_index + 2) % 4, axes=(1, 2)) for side_index in range(4)], 1)
    return (grad_padded[:, pad_depth:inner_end, pad_depth:inner_end], canon)

def strips_to_tiles(grad_strips, tile_side):
    pad_depth = grad_strips.shape[2]
    running = jnp.zeros((grad_strips.shape[0], tile_side, tile_side, grad_strips.shape[4]), jnp.float32)
    for quarter in range(4):
        placed = jnp.pad(grad_strips[:, quarter], ((0, 0), (0, tile_side - pad_depth), (0, 0), (0, 0)))
        running = running + jnp.rot90(placed, -quarter, axes=(1, 2))
    return running

def norm_parts(hidden, gain_vector):
    centered = hidden - lax.optimization_barrier(jnp.mean(hidden, -1, keepdims=True))
    inverse_scale = lax.rsqrt(lax.optimization_barrier(jnp.mean(centered * centered, -1, keepdims=True)) + 1e-06)
    standard = centered * inverse_scale
    return (standard, inverse_scale, (standard * gain_vector).astype(jnp.bfloat16))

def norm_back(grad_normed, standard, inverse_scale, gain_vector):
    scaled = grad_normed * gain_vector
    gain_grad = lax.optimization_barrier(jnp.sum(grad_normed * standard, 0))
    grad_hidden = inverse_scale * (scaled - lax.optimization_barrier(jnp.mean(scaled, -1, keepdims=True)) - standard * lax.optimization_barrier(jnp.mean(scaled * standard, -1, keepdims=True)))
    return (grad_hidden, gain_grad)

def grouped(inputs, weights, groups):
    group_width = inputs.shape[1] // groups
    running = jnp.zeros((inputs.shape[0], weights.shape[1]), jnp.float32)
    for group_index in range(groups):
        lower_end = group_index * group_width
        partial_value = jnp.dot(inputs[:, lower_end:lower_end + group_width], weights[lower_end:lower_end + group_width], preferred_element_type=jnp.float32).astype(jnp.bfloat16)
        partial_value = lax.optimization_barrier(partial_value)
        running = running + partial_value.astype(jnp.float32)
    return running

def reference(activations, cotangent, neighbours, rotations, kernels, gains, w_in, w_out):
    pad_depth = KS // 2
    pixels = TILES * S * S
    current = activations
    caches = []
    for layer_index in range(BLOCKS):
        padded = pad_tiles(current, neighbours, rotations, pad_depth)
        hidden = depthwise(padded, kernels[layer_index]).reshape(pixels, C)
        standard, inverse_scale, normed = norm_parts(hidden, gains[layer_index])
        linear_out = jnp.dot(normed, w_in[layer_index], preferred_element_type=jnp.float32)
        activated = jax.nn.gelu(linear_out).astype(jnp.bfloat16)
        caches.append((padded, standard, inverse_scale, normed, linear_out, activated))
        if layer_index + 1 < BLOCKS:
            mixed_sum = grouped(activated, w_out[layer_index], N_CHAN)
            current = (current.astype(jnp.float32) + mixed_sum.reshape(current.shape)).astype(jnp.bfloat16)
    gradient = cotangent.astype(jnp.float32).reshape(pixels, C)
    kernel_list, gain_list, in_list, out_list = ([None] * BLOCKS, [None] * BLOCKS, [None] * BLOCKS, [None] * BLOCKS)
    for layer_index in reversed(range(BLOCKS)):
        padded, standard, inverse_scale, normed, linear_out, activated = caches[layer_index]
        gradient_low = gradient.astype(jnp.bfloat16)
        grad_activated = jnp.dot(gradient_low, w_out[layer_index].T, preferred_element_type=jnp.float32)
        out_list[layer_index] = jnp.dot(activated.T, gradient_low, preferred_element_type=jnp.float32)
        gelu_back = jax.vjp(jax.nn.gelu, linear_out)[1]
        grad_linear = gelu_back(grad_activated)[0].astype(jnp.bfloat16)
        in_list[layer_index] = jnp.dot(normed.T, grad_linear, preferred_element_type=jnp.float32)
        grad_normed = grouped(grad_linear, w_in[layer_index].T, N_CHAN)
        grad_hidden, gain_list[layer_index] = norm_back(grad_normed, standard, inverse_scale, gains[layer_index])
        kernel_list[layer_index], grad_padded = depthwise_back(padded, grad_hidden.reshape(TILES, S, S, C), kernels[layer_index])
        interior, canon = side_canon(grad_padded, pad_depth)
        grad_strips = jnp.zeros(canon.shape, jnp.float32).at[neighbours, side_sources(rotations)].add(canon)
        gradient = (gradient.reshape(TILES, S, S, C) + (interior + strips_to_tiles(grad_strips, S))).reshape(pixels, C)
    input_grads = gradient.reshape(TILES, S, S, C).astype(jnp.bfloat16)
    return (input_grads, jnp.stack(kernel_list), jnp.stack(gain_list), jnp.stack(in_list), jnp.stack(out_list))
```

```python
import jax
import jax.numpy as jnp
import numpy as np
from jax import lax
from jax.experimental import pallas as pl
from jax.experimental.pallas import tpu as pltpu
from jax.sharding import PartitionSpec as P

BF = jnp.bfloat16
F32 = jnp.float32
KS = 7
PAD = 3
S = 16
EDGE = PAD * S
LANES = 128


def permutation_tables():
    pixel = np.arange(S * S).reshape(S, S)
    extract = np.zeros((4 * EDGE, S * S), np.float32)
    for quarter in range(4):
        source = np.rot90(pixel, quarter)[:PAD].reshape(-1)
        extract[quarter * EDGE + np.arange(EDGE), source] = 1
    strip = np.arange(EDGE).reshape(PAD, S)
    top = np.zeros((EDGE, EDGE), np.float32)
    top[np.arange(EDGE), np.rot90(strip, -2).reshape(-1)] = 1
    right = np.zeros((S, 8, EDGE), np.float32)
    left = np.zeros((S, 8, EDGE), np.float32)
    for i in range(S):
        for j in range(PAD):
            right[i, j, np.rot90(strip, -3)[i, j]] = 1
            left[i, 8 - PAD + j, np.rot90(strip, -1)[i, j]] = 1
    return extract, top, right.reshape(S * 8, EDGE), left.reshape(S * 8, EDGE)


def mm(a, b):
    return jnp.dot(a, b, preferred_element_type=F32)


def fill_shifted(x_ref, strips_ref, top_ref, right_ref, left_ref, pad_ref, sh_ref):
    @pl.when(pl.program_id(0) == 0)
    def _():
        pad_ref[...] = jnp.zeros_like(pad_ref)

    end = PAD + S
    pad_ref[PAD:end, 8:24] = x_ref[0].astype(F32)
    pad_ref[0:PAD, 8:24] = mm(top_ref[...], strips_ref[0, 0]).reshape(PAD, S, LANES)
    pad_ref[end:, 8:24] = strips_ref[0, 2].astype(F32).reshape(PAD, S, LANES)
    pad_ref[PAD:end, 24:32] = mm(right_ref[...], strips_ref[0, 1]).reshape(S, 8, LANES)
    pad_ref[PAD:end, 0:8] = mm(left_ref[...], strips_ref[0, 3]).reshape(S, 8, LANES)
    for b in range(KS):
        sh_ref[b] = pad_ref[:, 5 + b : 21 + b, :].reshape(S + 2 * PAD, 2, 8, LANES)


def depthwise(sh_ref, kern_ref, hid_ref):
    def body(block, carry):
        row = block * 4
        acc = jnp.zeros((4, 2, 8, LANES), F32)
        for b in range(KS):
            col = sh_ref[b, pl.ds(row, 4 + KS - 1)]
            for a in range(KS):
                acc = acc + col[a : a + 4] * kern_ref[b * KS + a][None, None]
        hid_ref[pl.ds(row, 4)] = acc
        return carry

    lax.fori_loop(0, S // 4, body, 0)


def normalise(hidden, gain):
    centered = hidden - jnp.mean(hidden, -1, keepdims=True)
    inverse = lax.rsqrt(jnp.mean(centered * centered, -1, keepdims=True) + 1e-06)
    standard = centered * inverse
    return standard, inverse, (standard * gain).astype(BF)


ROOT = 0.7978845608028654
CUBE = 0.044715


def forward_kernel(
    off_ref, x_ref, strips_ref, top_ref, right_ref, left_ref, extract_ref, kern_ref, gain_ref, w_in_ref, w_out_ref,
    hidden_ref, next_ref, next_strips_ref, pad_ref, sh_ref, hid_ref,
):
    fill_shifted(x_ref, strips_ref, top_ref, right_ref, left_ref, pad_ref, sh_ref)
    depthwise(sh_ref, kern_ref, hid_ref)
    hidden = hid_ref[...].reshape(S * S, LANES)
    hidden_ref[0] = hidden
    _, _, normed = normalise(hidden, gain_ref[...])
    linear = mm(normed, w_in_ref[...])
    act = 0.5 * linear * (1.0 + jnp.tanh(ROOT * (linear + CUBE * linear * linear * linear)))
    mixed = mm(act.astype(BF), w_out_ref[...])
    current = (x_ref[0].reshape(S * S, LANES).astype(F32) + mixed).astype(BF)
    next_ref[0] = current.reshape(S, S, LANES)
    next_strips_ref[0] = mm(extract_ref[...], current).astype(BF).reshape(4, EDGE, LANES)


def backward_kernel(
    first, x_ref, strips_ref, grad_ref, extra_ref, top_ref, right_ref, left_ref, place_ref, top_t_ref,
    right_t_ref, left_t_ref, kern_ref, gain_ref, w_in_ref, w_in_t_ref, w_out_t_ref,
    base_ref, canon_ref, kg_ref, gg_ref, wi_ref, wo_ref,
    pad_ref, sh_ref, hid_ref, gsh_ref, gh_ref, sum_ref, bl_ref, br_ref,
):
    @pl.when(pl.program_id(0) == 0)
    def _():
        kg_ref[...] = jnp.zeros_like(kg_ref)
        gg_ref[...] = jnp.zeros_like(gg_ref)
        wi_ref[...] = jnp.zeros_like(wi_ref)
        wo_ref[...] = jnp.zeros_like(wo_ref)
        gsh_ref[...] = jnp.zeros_like(gsh_ref)

    fill_shifted(x_ref, strips_ref, top_ref, right_ref, left_ref, pad_ref, sh_ref)
    if first:
        depthwise(sh_ref, kern_ref, hid_ref)
        hidden = hid_ref[...].reshape(S * S, LANES)
        gradient = grad_ref[0].reshape(S * S, LANES).astype(F32)
    else:
        hidden = extra_ref[0][0]
        gradient = grad_ref[0].reshape(S * S, LANES) + mm(
            place_ref[...], extra_ref[1][0].reshape(4 * EDGE, LANES)
        )
    sum_ref[...] = gradient.reshape(S, S, LANES)
    low = gradient.astype(BF)
    gain = gain_ref[...]
    standard, inverse, normed = normalise(hidden, gain)
    linear = mm(normed, w_in_ref[...])
    square = linear * linear
    tanh = jnp.tanh(ROOT * linear * (1.0 + CUBE * square))
    half = 0.5 * (1.0 + tanh)
    act = (linear * half).astype(BF)
    slope = half + linear * (0.5 * ROOT) * (1.0 - tanh * tanh) * (1.0 + (3.0 * CUBE) * square)
    grad_act = mm(low, w_out_t_ref[...])
    grad_linear = (slope * grad_act).astype(BF)
    over_pixels = (((0,), (0,)), ((), ()))
    wo_ref[...] += lax.dot_general(low, act, over_pixels, preferred_element_type=F32)
    wi_ref[...] += lax.dot_general(normed, grad_linear, over_pixels, preferred_element_type=F32)
    grad_normed = mm(grad_linear, w_in_t_ref[...])
    scaled = grad_normed * gain
    gg_ref[...] += jnp.sum((grad_normed * standard).reshape(S * S // 8, 8, LANES), 0)
    grad_hidden = inverse * (
        scaled
        - jnp.mean(scaled, -1, keepdims=True)
        - standard * jnp.mean(scaled * standard, -1, keepdims=True)
    )
    gh_ref[...] = grad_hidden.reshape(S, 2, 8, LANES)

    def column(b, carry):
        gh = gh_ref[...]
        for a in range(KS):
            kg_ref[b * KS + a] += jnp.sum(sh_ref[b, a : a + S] * gh, axis=(0, 1))
        taps = [kern_ref[b * KS + a][None] for a in range(KS)]
        for r in range(S + 2 * PAD):
            total = None
            for a in range(KS):
                if 0 <= r - a < S:
                    term = gh[r - a] * taps[a]
                    total = term if total is None else total + term
            gsh_ref[b, r, 16:32, :] = total.reshape(S, LANES)
        return carry

    lax.fori_loop(0, KS, column, 0)

    def rows(block, carry):
        row = block * 4
        total = gsh_ref[0, pl.ds(PAD + row, 4), 11:43, :]
        for b in range(1, KS):
            total = total + gsh_ref[b, pl.ds(PAD + row, 4), 11 - b : 43 - b, :]
        base_ref[0, pl.ds(row, 4)] = sum_ref[pl.ds(row, 4)] + total[:, 8:24]
        bl_ref[pl.ds(row, 4)] = total[:, 0:8]
        br_ref[pl.ds(row, 4)] = total[:, 24:32]
        return carry

    lax.fori_loop(0, S // 4, rows, 0)

    def outer(start):
        total = gsh_ref[0, start : start + PAD, 19:35, :]
        for b in range(1, KS):
            total = total + gsh_ref[b, start : start + PAD, 19 - b : 35 - b, :]
        return total.reshape(EDGE, LANES).astype(BF)

    canon_ref[0, 0] = mm(top_t_ref[...], outer(0)).astype(BF)
    canon_ref[0, 2] = outer(PAD + S)
    canon_ref[0, 1] = mm(right_t_ref[...], br_ref[...].reshape(S * 8, LANES).astype(BF)).astype(BF)
    canon_ref[0, 3] = mm(left_t_ref[...], bl_ref[...].reshape(S * 8, LANES).astype(BF)).astype(BF)


def whole(shape):
    return pl.BlockSpec(shape, lambda t, off: (0,) * len(shape))


def own_tile(shape, count):
    return pl.BlockSpec((1,) + shape, lambda t, off: (off[0] * count + t,) + (0,) * len(shape))


def each_tile(shape):
    return pl.BlockSpec((1,) + shape, lambda t, off: (t,) + (0,) * len(shape))


def shift_scratch():
    return [
        pltpu.VMEM((S + 2 * PAD, 32, LANES), F32),
        pltpu.VMEM((KS, S + 2 * PAD, 2, 8, LANES), F32),
        pltpu.VMEM((S, 2, 8, LANES), F32),
    ]


PARAMS = pltpu.CompilerParams(vmem_limit_bytes=40 * 1024 * 1024)


def forward_call(offset, count, x, strips, tables, kern, gain, w_in, w_out):
    hidden_units = w_in.shape[1]
    return pl.pallas_call(
        forward_kernel,
        grid_spec=pltpu.PrefetchScalarGridSpec(
            num_scalar_prefetch=1,
            grid=(count,),
            in_specs=[
                own_tile((S, S, LANES), count),
                each_tile((4, EDGE, LANES)),
                whole((EDGE, EDGE)),
                whole((S * 8, EDGE)),
                whole((S * 8, EDGE)),
                whole((4 * EDGE, S * S)),
                whole((KS * KS, 8, LANES)),
                whole((1, LANES)),
                whole((LANES, hidden_units)),
                whole((hidden_units, LANES)),
            ],
            out_specs=[
                each_tile((S * S, LANES)),
                each_tile((S, S, LANES)),
                each_tile((4, EDGE, LANES)),
            ],
            scratch_shapes=shift_scratch(),
        ),
        out_shape=[
            jax.ShapeDtypeStruct((count, S * S, LANES), F32),
            jax.ShapeDtypeStruct((count, S, S, LANES), BF),
            jax.ShapeDtypeStruct((count, 4, EDGE, LANES), BF),
        ],
        compiler_params=PARAMS,
        name="block_forward",
    )(offset, x, strips, *tables, kern, gain, w_in, w_out)


def first_backward(off_ref, x_ref, strips_ref, grad_ref, *rest):
    backward_kernel(True, x_ref, strips_ref, grad_ref, None, *rest)


def second_backward(off_ref, x_ref, strips_ref, grad_ref, hidden_ref, returned_ref, *rest):
    backward_kernel(False, x_ref, strips_ref, grad_ref, (hidden_ref, returned_ref), *rest)


def backward_call(first, offset, count, x, strips, grad, extra, tables, kern, gain, w_in, w_in_t, w_out_t):
    hidden_units = w_in.shape[1]
    x_spec = each_tile((S, S, LANES)) if first else own_tile((S, S, LANES), count)
    grad_spec = own_tile((S, S, LANES), count) if first else each_tile((S, S, LANES))
    extra_specs = [] if first else [each_tile((S * S, LANES)), each_tile((4, EDGE, LANES))]
    return pl.pallas_call(
        first_backward if first else second_backward,
        grid_spec=pltpu.PrefetchScalarGridSpec(
            num_scalar_prefetch=1,
            grid=(count,),
            in_specs=[x_spec, each_tile((4, EDGE, LANES)), grad_spec]
            + extra_specs
            + [whole(table.shape) for table in tables]
            + [
                whole((KS * KS, 8, LANES)),
                whole((1, LANES)),
                whole((LANES, hidden_units)),
                whole((hidden_units, LANES)),
                whole((LANES, hidden_units)),
            ],
            out_specs=[
                each_tile((S, S, LANES)),
                each_tile((4, EDGE, LANES)),
                whole((KS * KS, 8, LANES)),
                whole((8, LANES)),
                whole((LANES, hidden_units)),
                whole((LANES, hidden_units)),
            ],
            scratch_shapes=shift_scratch()
            + [
                pltpu.VMEM((KS, S + 2 * PAD, 48, LANES), F32),
                pltpu.VMEM((S, 2, 8, LANES), F32),
                pltpu.VMEM((S, S, LANES), F32),
                pltpu.VMEM((S, 8, LANES), F32),
                pltpu.VMEM((S, 8, LANES), F32),
            ],
        ),
        out_shape=[
            jax.ShapeDtypeStruct((count, S, S, LANES), F32),
            jax.ShapeDtypeStruct((count, 4, EDGE, LANES), BF),
            jax.ShapeDtypeStruct((KS * KS, 8, LANES), F32),
            jax.ShapeDtypeStruct((8, LANES), F32),
            jax.ShapeDtypeStruct((LANES, hidden_units), F32),
            jax.ShapeDtypeStruct((LANES, hidden_units), F32),
        ],
        compiler_params=PARAMS,
        name="block_backward",
    )(offset, x, strips, grad, *extra, *tables, kern, gain, w_in, w_in_t, w_out_t)


def shifted(value, axis, steps):
    count = lax.axis_size(axis)
    return lax.ppermute(value, axis, [(i, (i + steps) % count) for i in range(count)])


def swapped(value):
    return lax.ppermute(value, "chan", [(0, 1), (1, 0)])


def around(value):
    return shifted(value, "tile", 1), value, shifted(value, "tile", -1)


def exchange(strips):
    count = strips.shape[0]
    rows = strips.reshape(count * 4, EDGE * LANES)
    before, own, after = around(rows)
    mine = jnp.concatenate([before, own, after], 0)
    other = swapped(mine)
    return mine, other


def reduced(value, axis):
    count = lax.axis_size(axis)
    if count & (count - 1):
        return lax.psum(value.astype(BF), axis).astype(F32)
    step = 1
    while step < count:
        got = lax.ppermute(value.astype(BF), axis, [(i, i ^ step) for i in range(count)])
        value = value.astype(BF).astype(F32) + got.astype(F32)
        step *= 2
    return value


def local(activations, cotangent, neighbours, rotations, kernels, gains, w_in, w_out):
    tile_count = activations.shape[0]
    count = tile_count // 2
    chan = lax.axis_index("chan")
    position = lax.axis_index("tile")
    groups = lax.axis_size("tile")
    half_units = w_in.shape[2]
    offset = chan.astype(jnp.int32).reshape(1)

    extract, top, right, left = [jnp.asarray(table, BF) for table in permutation_tables()]
    forward_tables = (top, right, left, extract)
    backward_tables = (top, right, left, extract.T, top.T, right.T, left.T)

    seams = jnp.concatenate([neighbours, rotations], 1)
    seams_all = jnp.stack(around(seams), 0)

    own_first = lax.dynamic_slice_in_dim(activations, chan * count, count, 0)
    start_strips = jnp.einsum(
        "pk,tkc->tpc", extract, own_first.reshape(count, S * S, LANES), preferred_element_type=F32
    ).astype(BF)
    mine0, other0 = exchange(start_strips)

    joined = jnp.stack([w_in[0].T, w_in[1].T, w_out[0], w_out[1]], 0)
    gathered = lax.all_gather(joined, "chan", axis=1, tiled=True)
    in_t = [gathered[0], gathered[1]]
    out_w = [gathered[2], gathered[3]]
    in_w = [value.T for value in in_t]
    out_t = [value.T for value in out_w]
    taps = jnp.broadcast_to(
        kernels.astype(F32).transpose(0, 2, 1, 3).reshape(2, KS * KS, 1, LANES), (2, KS * KS, 8, LANES)
    )

    own_seams = lax.dynamic_slice_in_dim(seams, chan * count, count, 0)
    side = jnp.arange(4, dtype=jnp.int32)
    from_tile = own_seams[:, :4]
    source = (side[None, :] + 2 + own_seams[:, 4:]) % 4
    block_offset = (from_tile // tile_count - position + 1) % groups
    inner = from_tile % tile_count
    is_mine = (inner // count == chan).reshape(-1, 1)
    read_index = ((block_offset * count + inner % count) * 4 + source).reshape(-1)

    def choose(mine, other):
        picked = jnp.where(is_mine, jnp.take(mine, read_index, axis=0), jnp.take(other, read_index, axis=0))
        return picked.reshape(count, 4, EDGE, LANES)

    targets = seams_all[:, :, :4] * 4 + (side[None, None, :] + 2 + seams_all[:, :, 4:]) % 4
    targets_mine = lax.dynamic_slice_in_dim(targets, chan * count, count, 1).reshape(-1)
    targets_other = lax.dynamic_slice_in_dim(targets, (1 - chan) * count, count, 1).reshape(-1)
    slots = (position * tile_count + chan * count) * 4 + jnp.arange(count * 4, dtype=jnp.int32)
    hot_mine = (slots[:, None] == targets_mine[None, :]).astype(BF)
    hot_other = (slots[:, None] == targets_other[None, :]).astype(BF)

    def returned(canon):
        mine, other = exchange(canon)
        total = mm(hot_mine, mine) + mm(hot_other, other)
        return total.astype(BF).reshape(count, 4, EDGE, LANES)

    chosen0 = choose(mine0, other0)
    hidden0, current, strips1 = forward_call(
        offset, count, activations, chosen0, forward_tables, taps[0], gains[0:1], in_w[0], out_w[0]
    )
    chosen1 = choose(*exchange(strips1))
    base1, canon1, *grads1 = backward_call(
        True, offset, count, current, chosen1, cotangent, (), backward_tables,
        taps[1], gains[1:2], in_w[1], in_t[1], out_t[1],
    )

    def split(parts):
        kernel_part, gain_part, in_part, out_part = parts
        small = jnp.concatenate(
            [
                kernel_part.sum(1),
                gain_part.sum(0, keepdims=True),
            ],
            0,
        )
        stacked = jnp.stack([in_part, out_part], 0)

        def half(which):
            piece = lax.dynamic_slice_in_dim(stacked, which * half_units, half_units, 2)
            return jnp.concatenate([piece.reshape(-1, LANES), small], 0)

        total = half(chan) + swapped(half(1 - chan).astype(BF)).astype(F32)
        total = reduced(total, "tile")
        size = LANES * half_units // LANES
        kernel_sum = total[2 * size : 2 * size + KS * KS].reshape(KS, KS, LANES).transpose(1, 0, 2)
        return (
            kernel_sum,
            total[2 * size + KS * KS],
            total[:size].reshape(LANES, half_units),
            total[size : 2 * size].reshape(LANES, half_units).T,
        )

    sums1 = split(grads1)
    returned1 = returned(canon1)
    base0, canon0, *grads0 = backward_call(
        False, offset, count, activations, chosen0, base1, (hidden0, returned1), backward_tables,
        taps[0], gains[0:1], in_w[0], in_t[0], out_t[0],
    )
    returned0 = returned(canon0)
    sums0 = split(grads0)
    placed = jnp.einsum(
        "kp,tpc->tkc", extract.T, returned0.reshape(count, 4 * EDGE, LANES), preferred_element_type=F32
    )
    own_out = (base0 + placed.reshape(base0.shape)).astype(BF)
    input_grads = lax.all_gather(own_out, "chan", axis=0, tiled=True)
    stacked = [jnp.stack([a, b], 0) for a, b in zip(sums0, sums1)]
    return (input_grads, *stacked)


def solution(mesh):
    placed = (
        P(("parts", "tile"), None, None, None),
        P(("parts", "tile"), None, None, None),
        P("tile", None),
        P("tile", None),
        P(),
        P(),
        P(None, None, "chan"),
        P(None, "chan", None),
    )
    return jax.shard_map(
        local,
        mesh=mesh,
        in_specs=placed,
        out_specs=(
            P(("parts", "tile"), None, None, None),
            P("parts", None, None, None),
            P("parts", None),
            P("parts", None, "chan"),
            P("parts", "chan", None),
        ),
        check_vma=False,
    )
```

```python
import jax
import jax.numpy as jnp
import numpy as np
from jax import lax
from jax.experimental import pallas as pl
from jax.experimental.pallas import tpu as pltpu
from jax.sharding import PartitionSpec as P

BF = jnp.bfloat16
F32 = jnp.float32
KS = 7
PAD = 3
S = 16
EDGE = PAD * S
LANES = 128


def permutation_tables():
    pixel = np.arange(S * S).reshape(S, S)
    extract = np.zeros((4 * EDGE, S * S), np.float32)
    for quarter in range(4):
        source = np.rot90(pixel, quarter)[:PAD].reshape(-1)
        extract[quarter * EDGE + np.arange(EDGE), source] = 1
    strip = np.arange(EDGE).reshape(PAD, S)
    top = np.zeros((EDGE, EDGE), np.float32)
    top[np.arange(EDGE), np.rot90(strip, -2).reshape(-1)] = 1
    right = np.zeros((S, 8, EDGE), np.float32)
    left = np.zeros((S, 8, EDGE), np.float32)
    for i in range(S):
        for j in range(PAD):
            right[i, j, np.rot90(strip, -3)[i, j]] = 1
            left[i, 8 - PAD + j, np.rot90(strip, -1)[i, j]] = 1
    return extract, top, right.reshape(S * 8, EDGE), left.reshape(S * 8, EDGE)


def mm(a, b):
    return jnp.dot(a, b, preferred_element_type=F32)


def fill_shifted(x_ref, strips_ref, top_ref, right_ref, left_ref, pad_ref, sh_ref):
    @pl.when(pl.program_id(0) == 0)
    def _():
        pad_ref[...] = jnp.zeros_like(pad_ref)

    end = PAD + S
    pad_ref[PAD:end, 8:24] = x_ref[0].astype(F32)
    pad_ref[0:PAD, 8:24] = mm(top_ref[...], strips_ref[0, 0]).reshape(PAD, S, LANES)
    pad_ref[end:, 8:24] = strips_ref[0, 2].astype(F32).reshape(PAD, S, LANES)
    pad_ref[PAD:end, 24:32] = mm(right_ref[...], strips_ref[0, 1]).reshape(S, 8, LANES)
    pad_ref[PAD:end, 0:8] = mm(left_ref[...], strips_ref[0, 3]).reshape(S, 8, LANES)
    for b in range(KS):
        sh_ref[b] = pad_ref[:, 5 + b : 21 + b, :].reshape(S + 2 * PAD, 2, 8, LANES)


def depthwise(sh_ref, kern_ref, hid_ref):
    def body(block, carry):
        row = block * 4
        acc = jnp.zeros((4, 2, 8, LANES), F32)
        for b in range(KS):
            col = sh_ref[b, pl.ds(row, 4 + KS - 1)]
            for a in range(KS):
                acc = acc + col[a : a + 4] * kern_ref[b * KS + a][None, None]
        hid_ref[pl.ds(row, 4)] = acc
        return carry

    lax.fori_loop(0, S // 4, body, 0)


def normalise(hidden, gain):
    centered = hidden - jnp.mean(hidden, -1, keepdims=True)
    inverse = lax.rsqrt(jnp.mean(centered * centered, -1, keepdims=True) + 1e-06)
    standard = centered * inverse
    return standard, inverse, (standard * gain).astype(BF)


ROOT = 0.7978845608028654
CUBE = 0.044715


def forward_kernel(
    off_ref, x_ref, strips_ref, top_ref, right_ref, left_ref, extract_ref, kern_ref, gain_ref, w_in_ref, w_out_ref,
    hidden_ref, next_ref, next_strips_ref, pad_ref, sh_ref, hid_ref,
):
    fill_shifted(x_ref, strips_ref, top_ref, right_ref, left_ref, pad_ref, sh_ref)
    depthwise(sh_ref, kern_ref, hid_ref)
    hidden = hid_ref[...].reshape(S * S, LANES)
    hidden_ref[0] = hidden
    _, _, normed = normalise(hidden, gain_ref[...])
    linear = mm(normed, w_in_ref[...])
    act = 0.5 * linear * (1.0 + jnp.tanh(ROOT * (linear + CUBE * linear * linear * linear)))
    mixed = mm(act.astype(BF), w_out_ref[...])
    current = (x_ref[0].reshape(S * S, LANES).astype(F32) + mixed).astype(BF)
    next_ref[0] = current.reshape(S, S, LANES)
    next_strips_ref[0] = mm(extract_ref[...], current).astype(BF).reshape(4, EDGE, LANES)


def backward_kernel(
    first, x_ref, strips_ref, grad_ref, extra_ref, top_ref, right_ref, left_ref, place_ref, top_t_ref,
    right_t_ref, left_t_ref, kern_ref, gain_ref, w_in_ref, w_in_t_ref, w_out_t_ref,
    base_ref, canon_ref, kg_ref, gg_ref, wi_ref, wo_ref,
    pad_ref, sh_ref, hid_ref, gsh_ref, gh_ref, sum_ref, bl_ref, br_ref,
):
    @pl.when(pl.program_id(0) == 0)
    def _():
        kg_ref[...] = jnp.zeros_like(kg_ref)
        gg_ref[...] = jnp.zeros_like(gg_ref)
        wi_ref[...] = jnp.zeros_like(wi_ref)
        wo_ref[...] = jnp.zeros_like(wo_ref)
        gsh_ref[...] = jnp.zeros_like(gsh_ref)

    fill_shifted(x_ref, strips_ref, top_ref, right_ref, left_ref, pad_ref, sh_ref)
    if first:
        depthwise(sh_ref, kern_ref, hid_ref)
        hidden = hid_ref[...].reshape(S * S, LANES)
        gradient = grad_ref[0].reshape(S * S, LANES).astype(F32)
    else:
        hidden = extra_ref[0][0]
        gradient = grad_ref[0].reshape(S * S, LANES) + mm(
            place_ref[...], extra_ref[1][0].reshape(4 * EDGE, LANES)
        )
    sum_ref[...] = gradient.reshape(S, S, LANES)
    low = gradient.astype(BF)
    gain = gain_ref[...]
    standard, inverse, normed = normalise(hidden, gain)
    linear = mm(normed, w_in_ref[...])
    square = linear * linear
    tanh = jnp.tanh(ROOT * linear * (1.0 + CUBE * square))
    half = 0.5 * (1.0 + tanh)
    act = (linear * half).astype(BF)
    slope = half + linear * (0.5 * ROOT) * (1.0 - tanh * tanh) * (1.0 + (3.0 * CUBE) * square)
    grad_act = mm(low, w_out_t_ref[...])
    grad_linear = (slope * grad_act).astype(BF)
    over_pixels = (((0,), (0,)), ((), ()))
    wo_ref[...] += lax.dot_general(low, act, over_pixels, preferred_element_type=F32)
    wi_ref[...] += lax.dot_general(normed, grad_linear, over_pixels, preferred_element_type=F32)
    grad_normed = mm(grad_linear, w_in_t_ref[...])
    scaled = grad_normed * gain
    gg_ref[...] += jnp.sum((grad_normed * standard).reshape(S * S // 8, 8, LANES), 0)
    grad_hidden = inverse * (
        scaled
        - jnp.mean(scaled, -1, keepdims=True)
        - standard * jnp.mean(scaled * standard, -1, keepdims=True)
    )
    gh_ref[...] = grad_hidden.reshape(S, 2, 8, LANES)

    def column(b, carry):
        gh = gh_ref[...]
        for a in range(KS):
            kg_ref[b * KS + a] += jnp.sum(sh_ref[b, a : a + S] * gh, axis=(0, 1))
        taps = [kern_ref[b * KS + a][None] for a in range(KS)]
        for r in range(S + 2 * PAD):
            total = None
            for a in range(KS):
                if 0 <= r - a < S:
                    term = gh[r - a] * taps[a]
                    total = term if total is None else total + term
            gsh_ref[b, r, 16:32, :] = total.reshape(S, LANES)
        return carry

    lax.fori_loop(0, KS, column, 0)

    def rows(block, carry):
        row = block * 4
        total = gsh_ref[0, pl.ds(PAD + row, 4), 11:43, :]
        for b in range(1, KS):
            total = total + gsh_ref[b, pl.ds(PAD + row, 4), 11 - b : 43 - b, :]
        base_ref[0, pl.ds(row, 4)] = sum_ref[pl.ds(row, 4)] + total[:, 8:24]
        bl_ref[pl.ds(row, 4)] = total[:, 0:8]
        br_ref[pl.ds(row, 4)] = total[:, 24:32]
        return carry

    lax.fori_loop(0, S // 4, rows, 0)

    def outer(start):
        total = gsh_ref[0, start : start + PAD, 19:35, :]
        for b in range(1, KS):
            total = total + gsh_ref[b, start : start + PAD, 19 - b : 35 - b, :]
        return total.reshape(EDGE, LANES).astype(BF)

    canon_ref[0, 0] = mm(top_t_ref[...], outer(0)).astype(BF)
    canon_ref[0, 2] = outer(PAD + S)
    canon_ref[0, 1] = mm(right_t_ref[...], br_ref[...].reshape(S * 8, LANES).astype(BF)).astype(BF)
    canon_ref[0, 3] = mm(left_t_ref[...], bl_ref[...].reshape(S * 8, LANES).astype(BF)).astype(BF)


def whole(shape):
    return pl.BlockSpec(shape, lambda t, off: (0,) * len(shape))


def own_tile(shape, count):
    return pl.BlockSpec((1,) + shape, lambda t, off: (off[0] * count + t,) + (0,) * len(shape))


def each_tile(shape):
    return pl.BlockSpec((1,) + shape, lambda t, off: (t,) + (0,) * len(shape))


def shift_scratch():
    return [
        pltpu.VMEM((S + 2 * PAD, 32, LANES), F32),
        pltpu.VMEM((KS, S + 2 * PAD, 2, 8, LANES), F32),
        pltpu.VMEM((S, 2, 8, LANES), F32),
    ]


PARAMS = pltpu.CompilerParams(vmem_limit_bytes=40 * 1024 * 1024)


def forward_call(offset, count, x, strips, tables, kern, gain, w_in, w_out):
    hidden_units = w_in.shape[1]
    return pl.pallas_call(
        forward_kernel,
        grid_spec=pltpu.PrefetchScalarGridSpec(
            num_scalar_prefetch=1,
            grid=(count,),
            in_specs=[
                own_tile((S, S, LANES), count),
                each_tile((4, EDGE, LANES)),
                whole((EDGE, EDGE)),
                whole((S * 8, EDGE)),
                whole((S * 8, EDGE)),
                whole((4 * EDGE, S * S)),
                whole((KS * KS, 8, LANES)),
                whole((1, LANES)),
                whole((LANES, hidden_units)),
                whole((hidden_units, LANES)),
            ],
            out_specs=[
                each_tile((S * S, LANES)),
                each_tile((S, S, LANES)),
                each_tile((4, EDGE, LANES)),
            ],
            scratch_shapes=shift_scratch(),
        ),
        out_shape=[
            jax.ShapeDtypeStruct((count, S * S, LANES), F32),
            jax.ShapeDtypeStruct((count, S, S, LANES), BF),
            jax.ShapeDtypeStruct((count, 4, EDGE, LANES), BF),
        ],
        compiler_params=PARAMS,
        name="block_forward",
    )(offset, x, strips, *tables, kern, gain, w_in, w_out)


def first_backward(off_ref, x_ref, strips_ref, grad_ref, *rest):
    backward_kernel(True, x_ref, strips_ref, grad_ref, None, *rest)


def second_backward(off_ref, x_ref, strips_ref, grad_ref, hidden_ref, returned_ref, *rest):
    backward_kernel(False, x_ref, strips_ref, grad_ref, (hidden_ref, returned_ref), *rest)


def backward_call(first, offset, count, x, strips, grad, extra, tables, kern, gain, w_in, w_in_t, w_out_t):
    hidden_units = w_in.shape[1]
    x_spec = each_tile((S, S, LANES)) if first else own_tile((S, S, LANES), count)
    grad_spec = own_tile((S, S, LANES), count) if first else each_tile((S, S, LANES))
    extra_specs = [] if first else [each_tile((S * S, LANES)), each_tile((4, EDGE, LANES))]
    return pl.pallas_call(
        first_backward if first else second_backward,
        grid_spec=pltpu.PrefetchScalarGridSpec(
            num_scalar_prefetch=1,
            grid=(count,),
            in_specs=[x_spec, each_tile((4, EDGE, LANES)), grad_spec]
            + extra_specs
            + [whole(table.shape) for table in tables]
            + [
                whole((KS * KS, 8, LANES)),
                whole((1, LANES)),
                whole((LANES, hidden_units)),
                whole((hidden_units, LANES)),
                whole((LANES, hidden_units)),
            ],
            out_specs=[
                each_tile((S, S, LANES)),
                each_tile((4, EDGE, LANES)),
                whole((KS * KS, 8, LANES)),
                whole((8, LANES)),
                whole((LANES, hidden_units)),
                whole((LANES, hidden_units)),
            ],
            scratch_shapes=shift_scratch()
            + [
                pltpu.VMEM((KS, S + 2 * PAD, 48, LANES), F32),
                pltpu.VMEM((S, 2, 8, LANES), F32),
                pltpu.VMEM((S, S, LANES), F32),
                pltpu.VMEM((S, 8, LANES), F32),
                pltpu.VMEM((S, 8, LANES), F32),
            ],
        ),
        out_shape=[
            jax.ShapeDtypeStruct((count, S, S, LANES), F32),
            jax.ShapeDtypeStruct((count, 4, EDGE, LANES), BF),
            jax.ShapeDtypeStruct((KS * KS, 8, LANES), F32),
            jax.ShapeDtypeStruct((8, LANES), F32),
            jax.ShapeDtypeStruct((LANES, hidden_units), F32),
            jax.ShapeDtypeStruct((LANES, hidden_units), F32),
        ],
        compiler_params=PARAMS,
        name="block_backward",
    )(offset, x, strips, grad, *extra, *tables, kern, gain, w_in, w_in_t, w_out_t)


def shifted(value, axis, steps):
    count = lax.axis_size(axis)
    return lax.ppermute(value, axis, [(i, (i + steps) % count) for i in range(count)])


def swapped(value):
    return lax.ppermute(value, "chan", [(0, 1), (1, 0)])


def around(value):
    return shifted(value, "tile", 1), value, shifted(value, "tile", -1)


def ranked(mask):
    return jnp.cumsum(mask.astype(jnp.int32)) - 1


def picked(mask, values, first, width, empty):
    wanted = first + jnp.arange(width, dtype=jnp.int32)
    select = mask[None, :] & (ranked(mask)[None, :] == wanted[:, None])
    return jnp.max(jnp.where(select, values[None, :], empty), 1)


def in_rounds(rounds, body, state):
    return lax.while_loop(
        lambda carry: carry[0] < rounds,
        lambda carry: (carry[0] + 1, body(carry[0], carry[1])),
        (jnp.int32(1), state),
    )[1]


def reduced(value, axis):
    count = lax.axis_size(axis)
    if count & (count - 1):
        return lax.psum(value.astype(BF), axis).astype(F32)
    step = 1
    while step < count:
        got = lax.ppermute(value.astype(BF), axis, [(i, i ^ step) for i in range(count)])
        value = value.astype(BF).astype(F32) + got.astype(F32)
        step *= 2
    return value


def local(activations, cotangent, neighbours, rotations, kernels, gains, w_in, w_out):
    tile_count = activations.shape[0]
    count = tile_count // 2
    chan = lax.axis_index("chan")
    position = lax.axis_index("tile")
    groups = lax.axis_size("tile")
    half_units = w_in.shape[2]
    offset = chan.astype(jnp.int32).reshape(1)

    extract, top, right, left = [jnp.asarray(table, BF) for table in permutation_tables()]
    forward_tables = (top, right, left, extract)
    backward_tables = (top, right, left, extract.T, top.T, right.T, left.T)

    seams = jnp.concatenate([neighbours, rotations], 1)
    side = jnp.arange(4, dtype=jnp.int32)

    def sides_of(block_seams):
        part = lax.dynamic_slice_in_dim(block_seams, chan * count, count, 0)
        source = (side[None, :] + 2 + part[:, 4:]) % 4
        owner = part[:, :4] // tile_count
        slot = (part[:, :4] % tile_count) * 4 + source
        return owner.reshape(-1), slot.reshape(-1)

    def mine_first(slot):
        return slot % (count * 4) + jnp.where(slot // (count * 4) == chan, 0, count * 4)

    seams_before, _, seams_after = around(seams)
    owner, slot = sides_of(seams)
    owner_before, slot_before = sides_of(seams_before)
    owner_after, slot_after = sides_of(seams_after)
    to_before = owner == (position - 1) % groups
    to_after = owner == (position + 1) % groups
    within = owner == position
    from_before = owner_before == position
    from_after = owner_after == position
    most = jnp.maximum(jnp.sum(to_before.astype(jnp.int32)), jnp.sum(to_after.astype(jnp.int32)))
    rounds = (lax.pmax(most, ("parts", "tile", "chan")) + count - 1) // count

    strips0 = jnp.einsum(
        "pk,tkc->tpc", extract, activations.reshape(tile_count, S * S, LANES), preferred_element_type=F32
    ).astype(BF).reshape(tile_count * 4, EDGE * LANES)

    def fetch(full, place):
        def ask(index):
            for_after = picked(from_after, place(slot_after), index * count, count, 0)
            for_before = picked(from_before, place(slot_before), index * count, count, 0)
            return (
                shifted(jnp.take(full, for_after, axis=0), "tile", 1),
                shifted(jnp.take(full, for_before, axis=0), "tile", -1),
            )

        got_before, got_after = ask(0)
        table = jnp.concatenate([full, got_before, got_after], 0)
        last = count - 1
        base = full.shape[0]
        where_before = base + jnp.minimum(ranked(to_before), last)
        where_after = base + count + jnp.minimum(ranked(to_after), last)
        index = jnp.where(within, place(slot), jnp.where(to_before, where_before, where_after))
        chosen = jnp.take(table, index, axis=0)

        def more(index, chosen):
            got_before, got_after = ask(index)
            for mask, got in ((to_before, got_before), (to_after, got_after)):
                rank = ranked(mask) - index * count
                here = mask & (rank >= 0) & (rank < count)
                chosen = jnp.where(
                    here[:, None], jnp.take(got, jnp.clip(rank, 0, last), axis=0), chosen
                )
            return chosen

        return in_rounds(rounds, more, chosen).reshape(count, 4, EDGE, LANES)

    rows = jnp.arange(tile_count * 4, dtype=jnp.int32)[:, None]
    hot_within = (rows == jnp.where(within, mine_first(slot), -1)[None, :]).astype(BF)

    def returned(canon):
        canon = canon.reshape(count * 4, EDGE * LANES)
        numbers = jnp.arange(count * 4, dtype=jnp.int32)

        def send(index):
            for_before = picked(to_before, numbers, index * count, count, 0)
            for_after = picked(to_after, numbers, index * count, count, 0)
            aim_before = picked(from_before, mine_first(slot_before), index * count, count, -1)
            aim_after = picked(from_after, mine_first(slot_after), index * count, count, -1)
            got_before = shifted(jnp.take(canon, for_after, axis=0), "tile", 1)
            got_after = shifted(jnp.take(canon, for_before, axis=0), "tile", -1)
            aims = jnp.concatenate([aim_before, aim_after])
            return (rows == aims[None, :]).astype(BF), got_before, got_after

        hot, *got = send(0)
        total = mm(jnp.concatenate([hot_within, hot], 1), jnp.concatenate([canon, *got], 0))

        def more(index, total):
            hot, *got = send(index)
            return total + mm(hot, jnp.concatenate(got, 0))

        total = in_rounds(rounds, more, total)
        own, other = total[: count * 4], total[count * 4 :]
        total = own + swapped(other.astype(BF)).astype(F32)
        return total.astype(BF).reshape(count, 4, EDGE, LANES)

    joined = jnp.stack([w_in[0].T, w_in[1].T, w_out[0], w_out[1]], 0)
    gathered = lax.all_gather(joined, "chan", axis=1, tiled=True)
    in_t = [gathered[0], gathered[1]]
    out_w = [gathered[2], gathered[3]]
    in_w = [value.T for value in in_t]
    out_t = [value.T for value in out_w]
    taps = jnp.broadcast_to(
        kernels.astype(F32).transpose(0, 2, 1, 3).reshape(2, KS * KS, 1, LANES), (2, KS * KS, 8, LANES)
    )

    chosen0 = fetch(strips0, lambda value: value)
    hidden0, current, strips1 = forward_call(
        offset, count, activations, chosen0, forward_tables, taps[0], gains[0:1], in_w[0], out_w[0]
    )
    strips1 = strips1.reshape(count * 4, EDGE * LANES)
    chosen1 = fetch(jnp.concatenate([strips1, swapped(strips1)], 0), mine_first)
    base1, canon1, *grads1 = backward_call(
        True, offset, count, current, chosen1, cotangent, (), backward_tables,
        taps[1], gains[1:2], in_w[1], in_t[1], out_t[1],
    )

    def split(parts):
        kernel_part, gain_part, in_part, out_part = parts
        small = jnp.concatenate(
            [
                kernel_part.sum(1),
                gain_part.sum(0, keepdims=True),
            ],
            0,
        )
        stacked = jnp.stack([in_part, out_part], 0)

        def half(which):
            piece = lax.dynamic_slice_in_dim(stacked, which * half_units, half_units, 2)
            return jnp.concatenate([piece.reshape(-1, LANES), small], 0)

        total = half(chan) + swapped(half(1 - chan).astype(BF)).astype(F32)
        total = reduced(total, "tile")
        size = LANES * half_units // LANES
        kernel_sum = total[2 * size : 2 * size + KS * KS].reshape(KS, KS, LANES).transpose(1, 0, 2)
        return (
            kernel_sum,
            total[2 * size + KS * KS],
            total[:size].reshape(LANES, half_units),
            total[size : 2 * size].reshape(LANES, half_units).T,
        )

    sums1 = split(grads1)
    returned1 = returned(canon1)
    base0, canon0, *grads0 = backward_call(
        False, offset, count, activations, chosen0, base1, (hidden0, returned1), backward_tables,
        taps[0], gains[0:1], in_w[0], in_t[0], out_t[0],
    )
    returned0 = returned(canon0)
    sums0 = split(grads0)
    placed = jnp.einsum(
        "kp,tpc->tkc", extract.T, returned0.reshape(count, 4 * EDGE, LANES), preferred_element_type=F32
    )
    own_out = (base0 + placed.reshape(base0.shape)).astype(BF)
    input_grads = lax.all_gather(own_out, "chan", axis=0, tiled=True)
    stacked = [jnp.stack([a, b], 0) for a, b in zip(sums0, sums1)]
    return (input_grads, *stacked)


def solution(mesh):
    placed = (
        P(("parts", "tile"), None, None, None),
        P(("parts", "tile"), None, None, None),
        P("tile", None),
        P("tile", None),
        P(),
        P(),
        P(None, None, "chan"),
        P(None, "chan", None),
    )
    return jax.shard_map(
        local,
        mesh=mesh,
        in_specs=placed,
        out_specs=(
            P(("parts", "tile"), None, None, None),
            P("parts", None, None, None),
            P("parts", None),
            P("parts", None, "chan"),
            P("parts", "chan", None),
        ),
        check_vma=False,
    )
```

```python
import jax
import jax.numpy as jnp
import numpy as np
from jax import lax
from jax.experimental import pallas as pl
from jax.experimental.pallas import tpu as pltpu
from jax.sharding import PartitionSpec as P

BF = jnp.bfloat16
F32 = jnp.float32
KS = 7
PAD = 3
S = 16
EDGE = PAD * S
LANES = 128


def permutation_tables():
    pixel = np.arange(S * S).reshape(S, S)
    extract = np.zeros((4 * EDGE, S * S), np.float32)
    for quarter in range(4):
        source = np.rot90(pixel, quarter)[:PAD].reshape(-1)
        extract[quarter * EDGE + np.arange(EDGE), source] = 1
    strip = np.arange(EDGE).reshape(PAD, S)
    top = np.zeros((EDGE, EDGE), np.float32)
    top[np.arange(EDGE), np.rot90(strip, -2).reshape(-1)] = 1
    right = np.zeros((S, 8, EDGE), np.float32)
    left = np.zeros((S, 8, EDGE), np.float32)
    for i in range(S):
        for j in range(PAD):
            right[i, j, np.rot90(strip, -3)[i, j]] = 1
            left[i, 8 - PAD + j, np.rot90(strip, -1)[i, j]] = 1
    return extract, top, right.reshape(S * 8, EDGE), left.reshape(S * 8, EDGE)


def mm(a, b):
    return jnp.dot(a, b, preferred_element_type=F32)


def fill_shifted(info_ref, x_ref, strip_refs, top_ref, right_ref, left_ref, pad_ref, sh_ref):
    full_ref, before_ref, after_ref = strip_refs
    full_rows, more_rows = full_ref.shape[0], before_ref.shape[0]

    def strip(side):
        index = info_ref[1 + pl.program_id(0) * 4 + side]
        local = full_ref[jnp.minimum(index, full_rows - 1)].astype(F32)
        before = before_ref[jnp.clip(index - full_rows, 0, more_rows - 1)].astype(F32)
        after = after_ref[jnp.clip(index - full_rows - more_rows, 0, more_rows - 1)].astype(F32)
        return jnp.where(index < full_rows, local, jnp.where(index < full_rows + more_rows, before, after))

    @pl.when(pl.program_id(0) == 0)
    def _():
        pad_ref[...] = jnp.zeros_like(pad_ref)

    end = PAD + S
    pad_ref[PAD:end, 8:24] = x_ref[0].astype(F32)
    pad_ref[0:PAD, 8:24] = mm(top_ref[...], strip(0).astype(BF)).reshape(PAD, S, LANES)
    pad_ref[end:, 8:24] = strip(2).reshape(PAD, S, LANES)
    pad_ref[PAD:end, 24:32] = mm(right_ref[...], strip(1).astype(BF)).reshape(S, 8, LANES)
    pad_ref[PAD:end, 0:8] = mm(left_ref[...], strip(3).astype(BF)).reshape(S, 8, LANES)
    for b in range(KS):
        sh_ref[b] = pad_ref[:, 5 + b : 21 + b, :].reshape(S + 2 * PAD, 2, 8, LANES)


def depthwise(sh_ref, kern_ref, hid_ref):
    def body(block, carry):
        row = block * 4
        acc = jnp.zeros((4, 2, 8, LANES), F32)
        for b in range(KS):
            col = sh_ref[b, pl.ds(row, 4 + KS - 1)]
            for a in range(KS):
                acc = acc + col[a : a + 4] * kern_ref[b * KS + a][None, None]
        hid_ref[pl.ds(row, 4)] = acc
        return carry

    lax.fori_loop(0, S // 4, body, 0)


def normalise(hidden, gain):
    centered = hidden - jnp.mean(hidden, -1, keepdims=True)
    inverse = lax.rsqrt(jnp.mean(centered * centered, -1, keepdims=True) + 1e-06)
    standard = centered * inverse
    return standard, inverse, (standard * gain).astype(BF)


ROOT = 0.7978845608028654
CUBE = 0.044715


def forward_kernel(
    info_ref, x_ref, full_ref, before_ref, after_ref, top_ref, right_ref, left_ref, extract_ref, kern_ref, gain_ref, w_in_ref, w_out_ref,
    hidden_ref, next_ref, next_strips_ref, pad_ref, sh_ref, hid_ref,
):
    strip_refs = (full_ref, before_ref, after_ref)
    fill_shifted(info_ref, x_ref, strip_refs, top_ref, right_ref, left_ref, pad_ref, sh_ref)
    depthwise(sh_ref, kern_ref, hid_ref)
    hidden = hid_ref[...].reshape(S * S, LANES)
    hidden_ref[0] = hidden
    _, _, normed = normalise(hidden, gain_ref[...])
    linear = mm(normed, w_in_ref[...])
    act = 0.5 * linear * (1.0 + jnp.tanh(ROOT * (linear + CUBE * linear * linear * linear)))
    mixed = mm(act.astype(BF), w_out_ref[...])
    current = (x_ref[0].reshape(S * S, LANES).astype(F32) + mixed).astype(BF)
    next_ref[0] = current.reshape(S, S, LANES)
    next_strips_ref[0] = mm(extract_ref[...], current).astype(BF).reshape(4, EDGE, LANES)


def backward_kernel(
    first, info_ref, x_ref, strip_refs, grad_ref, extra_ref, top_ref, right_ref, left_ref, place_ref, top_t_ref,
    right_t_ref, left_t_ref, kern_ref, gain_ref, w_in_ref, w_in_t_ref, w_out_t_ref,
    base_ref, canon_ref, kg_ref, gg_ref, wi_ref, wo_ref,
    pad_ref, sh_ref, hid_ref, gsh_ref, gh_ref, sum_ref, bl_ref, br_ref,
):
    @pl.when(pl.program_id(0) == 0)
    def _():
        kg_ref[...] = jnp.zeros_like(kg_ref)
        gg_ref[...] = jnp.zeros_like(gg_ref)
        wi_ref[...] = jnp.zeros_like(wi_ref)
        wo_ref[...] = jnp.zeros_like(wo_ref)
        gsh_ref[...] = jnp.zeros_like(gsh_ref)

    fill_shifted(info_ref, x_ref, strip_refs, top_ref, right_ref, left_ref, pad_ref, sh_ref)
    if first:
        depthwise(sh_ref, kern_ref, hid_ref)
        hidden = hid_ref[...].reshape(S * S, LANES)
        gradient = grad_ref[0].reshape(S * S, LANES).astype(F32)
    else:
        hidden = extra_ref[0][0]
        back = (extra_ref[1][...] + extra_ref[2][...].astype(F32)).astype(BF)
        gradient = grad_ref[0].reshape(S * S, LANES) + mm(
            place_ref[...], back.reshape(4 * EDGE, LANES)
        )
    sum_ref[...] = gradient.reshape(S, S, LANES)
    low = gradient.astype(BF)
    gain = gain_ref[...]
    standard, inverse, normed = normalise(hidden, gain)
    linear = mm(normed, w_in_ref[...])
    square = linear * linear
    tanh = jnp.tanh(ROOT * linear * (1.0 + CUBE * square))
    half = 0.5 * (1.0 + tanh)
    act = (linear * half).astype(BF)
    slope = half + linear * (0.5 * ROOT) * (1.0 - tanh * tanh) * (1.0 + (3.0 * CUBE) * square)
    grad_act = mm(low, w_out_t_ref[...])
    grad_linear = (slope * grad_act).astype(BF)
    over_pixels = (((0,), (0,)), ((), ()))
    wo_ref[...] += lax.dot_general(low, act, over_pixels, preferred_element_type=F32)
    wi_ref[...] += lax.dot_general(normed, grad_linear, over_pixels, preferred_element_type=F32)
    grad_normed = mm(grad_linear, w_in_t_ref[...])
    scaled = grad_normed * gain
    gg_ref[...] += jnp.sum((grad_normed * standard).reshape(S * S // 8, 8, LANES), 0)
    grad_hidden = inverse * (
        scaled
        - jnp.mean(scaled, -1, keepdims=True)
        - standard * jnp.mean(scaled * standard, -1, keepdims=True)
    )
    gh_ref[...] = grad_hidden.reshape(S, 2, 8, LANES)

    def column(b, carry):
        gh = gh_ref[...]
        for a in range(KS):
            kg_ref[b * KS + a] += jnp.sum(sh_ref[b, a : a + S] * gh, axis=(0, 1))
        taps = [kern_ref[b * KS + a][None] for a in range(KS)]
        for r in range(S + 2 * PAD):
            total = None
            for a in range(KS):
                if 0 <= r - a < S:
                    term = gh[r - a] * taps[a]
                    total = term if total is None else total + term
            gsh_ref[b, r, 16:32, :] = total.reshape(S, LANES)
        return carry

    lax.fori_loop(0, KS, column, 0)

    def rows(block, carry):
        row = block * 4
        total = gsh_ref[0, pl.ds(PAD + row, 4), 11:43, :]
        for b in range(1, KS):
            total = total + gsh_ref[b, pl.ds(PAD + row, 4), 11 - b : 43 - b, :]
        base_ref[0, pl.ds(row, 4)] = sum_ref[pl.ds(row, 4)] + total[:, 8:24]
        bl_ref[pl.ds(row, 4)] = total[:, 0:8]
        br_ref[pl.ds(row, 4)] = total[:, 24:32]
        return carry

    lax.fori_loop(0, S // 4, rows, 0)

    def outer(start):
        total = gsh_ref[0, start : start + PAD, 19:35, :]
        for b in range(1, KS):
            total = total + gsh_ref[b, start : start + PAD, 19 - b : 35 - b, :]
        return total.reshape(EDGE, LANES).astype(BF)

    canon_ref[0, 0] = mm(top_t_ref[...], outer(0)).astype(BF)
    canon_ref[0, 2] = outer(PAD + S)
    canon_ref[0, 1] = mm(right_t_ref[...], br_ref[...].reshape(S * 8, LANES).astype(BF)).astype(BF)
    canon_ref[0, 3] = mm(left_t_ref[...], bl_ref[...].reshape(S * 8, LANES).astype(BF)).astype(BF)


def whole(shape):
    return pl.BlockSpec(shape, lambda t, off: (0,) * len(shape))


def own_tile(shape, count):
    return pl.BlockSpec((1,) + shape, lambda t, off: (off[0] * count + t,) + (0,) * len(shape))


def each_tile(shape):
    return pl.BlockSpec((1,) + shape, lambda t, off: (t,) + (0,) * len(shape))


def shift_scratch():
    return [
        pltpu.VMEM((S + 2 * PAD, 32, LANES), F32),
        pltpu.VMEM((KS, S + 2 * PAD, 2, 8, LANES), F32),
        pltpu.VMEM((S, 2, 8, LANES), F32),
    ]


PARAMS = pltpu.CompilerParams(vmem_limit_bytes=40 * 1024 * 1024)


def forward_call(info, count, x, strips, tables, kern, gain, w_in, w_out):
    hidden_units = w_in.shape[1]
    return pl.pallas_call(
        forward_kernel,
        grid_spec=pltpu.PrefetchScalarGridSpec(
            num_scalar_prefetch=1,
            grid=(count,),
            in_specs=[
                own_tile((S, S, LANES), count),
                *[whole(part.shape) for part in strips],
                whole((EDGE, EDGE)),
                whole((S * 8, EDGE)),
                whole((S * 8, EDGE)),
                whole((4 * EDGE, S * S)),
                whole((KS * KS, 8, LANES)),
                whole((1, LANES)),
                whole((LANES, hidden_units)),
                whole((hidden_units, LANES)),
            ],
            out_specs=[
                each_tile((S * S, LANES)),
                each_tile((S, S, LANES)),
                each_tile((4, EDGE, LANES)),
            ],
            scratch_shapes=shift_scratch(),
        ),
        out_shape=[
            jax.ShapeDtypeStruct((count, S * S, LANES), F32),
            jax.ShapeDtypeStruct((count, S, S, LANES), BF),
            jax.ShapeDtypeStruct((count, 4, EDGE, LANES), BF),
        ],
        compiler_params=PARAMS,
        name="block_forward",
    )(info, x, *strips, *tables, kern, gain, w_in, w_out)


def first_backward(info_ref, x_ref, full_ref, before_ref, after_ref, grad_ref, *rest):
    backward_kernel(True, info_ref, x_ref, (full_ref, before_ref, after_ref), grad_ref, None, *rest)


def second_backward(
    info_ref, x_ref, full_ref, before_ref, after_ref, grad_ref, hidden_ref, own_ref, other_ref, *rest
):
    strip_refs = (full_ref, before_ref, after_ref)
    backward_kernel(False, info_ref, x_ref, strip_refs, grad_ref, (hidden_ref, own_ref, other_ref), *rest)


def collect_kernel(aims_ref, canon_ref, before_ref, after_ref, total_ref):
    total_ref[...] = jnp.zeros_like(total_ref)
    start = 0
    for source_ref in (canon_ref, before_ref, after_ref):

        def body(k, carry, source_ref=source_ref, start=start):
            aim = aims_ref[start + k]

            @pl.when(aim >= 0)
            def _():
                place = jnp.maximum(aim, 0)
                total_ref[place] = total_ref[place] + source_ref[k].astype(F32)

            return carry

        lax.fori_loop(0, source_ref.shape[0], body, 0)
        start += source_ref.shape[0]


def collect_call(aims, canon, before, after):
    rows = 2 * canon.shape[0]
    return pl.pallas_call(
        collect_kernel,
        grid_spec=pltpu.PrefetchScalarGridSpec(
            num_scalar_prefetch=1,
            grid=(1,),
            in_specs=[whole(canon.shape), whole(before.shape), whole(after.shape)],
            out_specs=whole((rows, EDGE, LANES)),
        ),
        out_shape=jax.ShapeDtypeStruct((rows, EDGE, LANES), F32),
        compiler_params=PARAMS,
        name="collect_strips",
    )(aims, canon, before, after)


def backward_call(first, info, count, x, strips, grad, extra, tables, kern, gain, w_in, w_in_t, w_out_t):
    hidden_units = w_in.shape[1]
    x_spec = each_tile((S, S, LANES)) if first else own_tile((S, S, LANES), count)
    grad_spec = own_tile((S, S, LANES), count) if first else each_tile((S, S, LANES))
    four = pl.BlockSpec((4, EDGE, LANES), lambda t, off: (t, 0, 0))
    extra_specs = [] if first else [each_tile((S * S, LANES)), four, four]
    return pl.pallas_call(
        first_backward if first else second_backward,
        grid_spec=pltpu.PrefetchScalarGridSpec(
            num_scalar_prefetch=1,
            grid=(count,),
            in_specs=[x_spec, *[whole(part.shape) for part in strips], grad_spec]
            + extra_specs
            + [whole(table.shape) for table in tables]
            + [
                whole((KS * KS, 8, LANES)),
                whole((1, LANES)),
                whole((LANES, hidden_units)),
                whole((hidden_units, LANES)),
                whole((LANES, hidden_units)),
            ],
            out_specs=[
                each_tile((S, S, LANES)),
                each_tile((4, EDGE, LANES)),
                whole((KS * KS, 8, LANES)),
                whole((8, LANES)),
                whole((LANES, hidden_units)),
                whole((LANES, hidden_units)),
            ],
            scratch_shapes=shift_scratch()
            + [
                pltpu.VMEM((KS, S + 2 * PAD, 48, LANES), F32),
                pltpu.VMEM((S, 2, 8, LANES), F32),
                pltpu.VMEM((S, S, LANES), F32),
                pltpu.VMEM((S, 8, LANES), F32),
                pltpu.VMEM((S, 8, LANES), F32),
            ],
        ),
        out_shape=[
            jax.ShapeDtypeStruct((count, S, S, LANES), F32),
            jax.ShapeDtypeStruct((count, 4, EDGE, LANES), BF),
            jax.ShapeDtypeStruct((KS * KS, 8, LANES), F32),
            jax.ShapeDtypeStruct((8, LANES), F32),
            jax.ShapeDtypeStruct((LANES, hidden_units), F32),
            jax.ShapeDtypeStruct((LANES, hidden_units), F32),
        ],
        compiler_params=PARAMS,
        name="block_backward",
    )(info, x, *strips, grad, *extra, *tables, kern, gain, w_in, w_in_t, w_out_t)


def shifted(value, axis, steps):
    count = lax.axis_size(axis)
    return lax.ppermute(value, axis, [(i, (i + steps) % count) for i in range(count)])


def swapped(value):
    return lax.ppermute(value, "chan", [(0, 1), (1, 0)])


def around(value):
    return shifted(value, "tile", 1), value, shifted(value, "tile", -1)


def ranked(mask):
    return jnp.cumsum(mask.astype(jnp.int32)) - 1


def picked(mask, values, first, width, empty):
    wanted = first + jnp.arange(width, dtype=jnp.int32)
    select = mask[None, :] & (ranked(mask)[None, :] == wanted[:, None])
    return jnp.max(jnp.where(select, values[None, :], empty), 1)


def in_rounds(rounds, body, state):
    return lax.while_loop(
        lambda carry: carry[0] < rounds,
        lambda carry: (carry[0] + 1, body(carry[0], carry[1])),
        (jnp.int32(1), state),
    )[1]


def highest(value, axis):
    count = lax.axis_size(axis)
    if count & (count - 1):
        return lax.pmax(value, axis)
    step = 1
    while step < count:
        value = jnp.maximum(value, lax.ppermute(value, axis, [(i, i ^ step) for i in range(count)]))
        step *= 2
    return value


def reduced(value, axis):
    count = lax.axis_size(axis)
    if count & (count - 1):
        return lax.psum(value.astype(BF), axis).astype(F32)
    step = 1
    while step < count:
        got = lax.ppermute(value.astype(BF), axis, [(i, i ^ step) for i in range(count)])
        value = value.astype(BF).astype(F32) + got.astype(F32)
        step *= 2
    return value


def local(activations, cotangent, neighbours, rotations, kernels, gains, w_in, w_out):
    tile_count = activations.shape[0]
    count = tile_count // 2
    chan = lax.axis_index("chan")
    position = lax.axis_index("tile")
    groups = lax.axis_size("tile")
    half_units = w_in.shape[2]

    extract, top, right, left = [jnp.asarray(table, BF) for table in permutation_tables()]
    forward_tables = (top, right, left, extract)
    backward_tables = (top, right, left, extract.T, top.T, right.T, left.T)

    seams = jnp.concatenate([neighbours, rotations], 1)
    side = jnp.arange(4, dtype=jnp.int32)

    def sides_of(block_seams):
        part = lax.dynamic_slice_in_dim(block_seams, chan * count, count, 0)
        source = (side[None, :] + 2 + part[:, 4:]) % 4
        owner = part[:, :4] // tile_count
        slot = (part[:, :4] % tile_count) * 4 + source
        return owner.reshape(-1), slot.reshape(-1)

    def mine_first(slot):
        return slot % (count * 4) + jnp.where(slot // (count * 4) == chan, 0, count * 4)

    seams_before, _, seams_after = around(seams)
    owner, slot = sides_of(seams)
    owner_before, slot_before = sides_of(seams_before)
    owner_after, slot_after = sides_of(seams_after)
    to_before = owner == (position - 1) % groups
    to_after = owner == (position + 1) % groups
    within = owner == position
    from_before = owner_before == position
    from_after = owner_after == position
    owners = (neighbours // tile_count).reshape(2, count * 4)
    before_count = jnp.sum((owners == (position - 1) % groups).astype(jnp.int32), 1)
    after_count = jnp.sum((owners == (position + 1) % groups).astype(jnp.int32), 1)
    most = jnp.broadcast_to(jnp.max(jnp.maximum(before_count, after_count)), (LANES,))
    rounds = (highest(most, "tile")[0] + count - 1) // count

    strips0 = jnp.einsum(
        "pk,tkc->tpc", extract, activations.reshape(tile_count, S * S, LANES), preferred_element_type=F32
    ).astype(BF).reshape(tile_count * 4, EDGE, LANES)

    def fetch(full, place):
        def ask(index):
            for_after = picked(from_after, place(slot_after), index * count, count, 0)
            for_before = picked(from_before, place(slot_before), index * count, count, 0)
            return (
                shifted(jnp.take(full, for_after, axis=0), "tile", 1),
                shifted(jnp.take(full, for_before, axis=0), "tile", -1),
            )

        def widened(got):
            return jnp.pad(got, ((0, 3 * count), (0, 0), (0, 0)))

        def more(index, state):
            return tuple(
                lax.dynamic_update_slice_in_dim(held, got, index * count, 0)
                for held, got in zip(state, ask(index))
            )

        before, after = in_rounds(rounds, more, tuple(widened(got) for got in ask(0)))
        base = full.shape[0]
        where_before = base + ranked(to_before)
        where_after = base + 4 * count + ranked(to_after)
        index = jnp.where(within, place(slot), jnp.where(to_before, where_before, where_after))
        return jnp.concatenate([chan.astype(jnp.int32).reshape(1), index]), (full, before, after)

    aim_within = jnp.where(within, mine_first(slot), -1)

    def returned(canon):
        canon = canon.reshape(count * 4, EDGE, LANES)
        numbers = jnp.arange(count * 4, dtype=jnp.int32)

        def send(index):
            for_before = picked(to_before, numbers, index * count, count, 0)
            for_after = picked(to_after, numbers, index * count, count, 0)
            aim_before = picked(from_before, mine_first(slot_before), index * count, count, -1)
            aim_after = picked(from_after, mine_first(slot_after), index * count, count, -1)
            got_before = shifted(jnp.take(canon, for_after, axis=0), "tile", 1)
            got_after = shifted(jnp.take(canon, for_before, axis=0), "tile", -1)
            return jnp.concatenate([aim_before, aim_after]), got_before, got_after

        aims, got_before, got_after = send(0)
        total = collect_call(jnp.concatenate([aim_within, aims]), canon, got_before, got_after)

        def more(index, total):
            aims, *got = send(index)
            aims = jnp.where(aims < 0, tile_count * 4, aims)
            return total.at[aims].add(jnp.concatenate(got, 0).astype(F32), mode="drop")

        total = in_rounds(rounds, more, total)
        return total, swapped(total[count * 4 :].astype(BF))

    joined = jnp.stack([w_in[0].T, w_in[1].T, w_out[0], w_out[1]], 0)
    gathered = lax.all_gather(joined, "chan", axis=1, tiled=True)
    in_t = [gathered[0], gathered[1]]
    out_w = [gathered[2], gathered[3]]
    in_w = [value.T for value in in_t]
    out_t = [value.T for value in out_w]
    taps = jnp.broadcast_to(
        kernels.astype(F32).transpose(0, 2, 1, 3).reshape(2, KS * KS, 1, LANES), (2, KS * KS, 8, LANES)
    )

    info0, chosen0 = fetch(strips0, lambda value: value)
    hidden0, current, strips1 = forward_call(
        info0, count, activations, chosen0, forward_tables, taps[0], gains[0:1], in_w[0], out_w[0]
    )
    strips1 = strips1.reshape(count * 4, EDGE, LANES)
    info1, chosen1 = fetch(jnp.concatenate([strips1, swapped(strips1)], 0), mine_first)
    base1, canon1, *grads1 = backward_call(
        True, info1, count, current, chosen1, cotangent, (), backward_tables,
        taps[1], gains[1:2], in_w[1], in_t[1], out_t[1],
    )

    def split(parts):
        kernel_part, gain_part, in_part, out_part = parts
        small = jnp.concatenate(
            [
                kernel_part.sum(1),
                gain_part.sum(0, keepdims=True),
            ],
            0,
        )
        stacked = jnp.stack([in_part, out_part], 0)

        def half(which):
            piece = lax.dynamic_slice_in_dim(stacked, which * half_units, half_units, 2)
            return jnp.concatenate([piece.reshape(-1, LANES), small], 0)

        total = half(chan) + swapped(half(1 - chan).astype(BF)).astype(F32)
        total = reduced(total, "tile")
        size = LANES * half_units // LANES
        kernel_sum = total[2 * size : 2 * size + KS * KS].reshape(KS, KS, LANES).transpose(1, 0, 2)
        return (
            kernel_sum,
            total[2 * size + KS * KS],
            total[:size].reshape(LANES, half_units),
            total[size : 2 * size].reshape(LANES, half_units).T,
        )

    sums1 = split(grads1)
    returned1 = returned(canon1)
    base0, canon0, *grads0 = backward_call(
        False, info0, count, activations, chosen0, base1, (hidden0, *returned1), backward_tables,
        taps[0], gains[0:1], in_w[0], in_t[0], out_t[0],
    )
    own0, other0 = returned(canon0)
    returned0 = (own0[: count * 4] + other0.astype(F32)).astype(BF)
    sums0 = split(grads0)
    placed = jnp.einsum(
        "kp,tpc->tkc", extract.T, returned0.reshape(count, 4 * EDGE, LANES), preferred_element_type=F32
    )
    own_out = (base0 + placed.reshape(base0.shape)).astype(BF)
    input_grads = lax.all_gather(own_out, "chan", axis=0, tiled=True)
    stacked = [jnp.stack([a, b], 0) for a, b in zip(sums0, sums1)]
    return (input_grads, *stacked)


def solution(mesh):
    placed = (
        P(("parts", "tile"), None, None, None),
        P(("parts", "tile"), None, None, None),
        P("tile", None),
        P("tile", None),
        P(),
        P(),
        P(None, None, "chan"),
        P(None, "chan", None),
    )
    return jax.shard_map(
        local,
        mesh=mesh,
        in_specs=placed,
        out_specs=(
            P(("parts", "tile"), None, None, None),
            P("parts", None, None, None),
            P("parts", None),
            P("parts", None, "chan"),
            P("parts", "chan", None),
        ),
        check_vma=False,
    )
```

```python
import jax
import jax.numpy as jnp
import numpy as np
from jax import lax
from jax.experimental import pallas as pl
from jax.experimental.pallas import tpu as pltpu
from jax.sharding import PartitionSpec as P

BF = jnp.bfloat16
F32 = jnp.float32
KS = 7
PAD = 3
S = 16
EDGE = PAD * S
LANES = 128


def permutation_tables():
    pixel = np.arange(S * S).reshape(S, S)
    extract = np.zeros((4 * EDGE, S * S), np.float32)
    for quarter in range(4):
        source = np.rot90(pixel, quarter)[:PAD].reshape(-1)
        extract[quarter * EDGE + np.arange(EDGE), source] = 1
    strip = np.arange(EDGE).reshape(PAD, S)
    top = np.zeros((EDGE, EDGE), np.float32)
    top[np.arange(EDGE), np.rot90(strip, -2).reshape(-1)] = 1
    right = np.zeros((S, 8, EDGE), np.float32)
    left = np.zeros((S, 8, EDGE), np.float32)
    for i in range(S):
        for j in range(PAD):
            right[i, j, np.rot90(strip, -3)[i, j]] = 1
            left[i, 8 - PAD + j, np.rot90(strip, -1)[i, j]] = 1
    return extract, top, right.reshape(S * 8, EDGE), left.reshape(S * 8, EDGE)


def mm(a, b):
    return jnp.dot(a, b, preferred_element_type=F32)


def fill_shifted(info_ref, x_ref, strip_refs, top_ref, right_ref, left_ref, pad_ref, sh_ref):
    full_ref, before_ref, after_ref = strip_refs
    full_rows, more_rows = full_ref.shape[0], before_ref.shape[0]

    def strip(side):
        index = info_ref[1 + pl.program_id(0) * 4 + side]
        local = full_ref[jnp.minimum(index, full_rows - 1)].astype(F32)
        before = before_ref[jnp.clip(index - full_rows, 0, more_rows - 1)].astype(F32)
        after = after_ref[jnp.clip(index - full_rows - more_rows, 0, more_rows - 1)].astype(F32)
        return jnp.where(index < full_rows, local, jnp.where(index < full_rows + more_rows, before, after))

    @pl.when(pl.program_id(0) == 0)
    def _():
        pad_ref[...] = jnp.zeros_like(pad_ref)

    end = PAD + S
    pad_ref[PAD:end, 8:24] = x_ref[0].astype(F32)
    pad_ref[0:PAD, 8:24] = mm(top_ref[...], strip(0).astype(BF)).reshape(PAD, S, LANES)
    pad_ref[end:, 8:24] = strip(2).reshape(PAD, S, LANES)
    pad_ref[PAD:end, 24:32] = mm(right_ref[...], strip(1).astype(BF)).reshape(S, 8, LANES)
    pad_ref[PAD:end, 0:8] = mm(left_ref[...], strip(3).astype(BF)).reshape(S, 8, LANES)
    for b in range(KS):
        sh_ref[b] = pad_ref[:, 5 + b : 21 + b, :].reshape(S + 2 * PAD, 2, 8, LANES)


def depthwise(sh_ref, kern_ref, hid_ref):
    def body(block, carry):
        row = block * 4
        acc = jnp.zeros((4, 2, 8, LANES), F32)
        for b in range(KS):
            col = sh_ref[b, pl.ds(row, 4 + KS - 1)]
            for a in range(KS):
                acc = acc + col[a : a + 4] * kern_ref[b * KS + a][None, None]
        hid_ref[pl.ds(row, 4)] = acc
        return carry

    lax.fori_loop(0, S // 4, body, 0)


def normalise(hidden, gain):
    centered = hidden - jnp.mean(hidden, -1, keepdims=True)
    inverse = lax.rsqrt(jnp.mean(centered * centered, -1, keepdims=True) + 1e-06)
    standard = centered * inverse
    return standard, inverse, (standard * gain).astype(BF)


ROOT = 0.7978845608028654
CUBE = 0.044715


def forward_kernel(
    info_ref, x_ref, full_ref, before_ref, after_ref, top_ref, right_ref, left_ref, extract_ref, kern_ref, gain_ref, w_in_ref, w_out_ref,
    hidden_ref, next_ref, next_strips_ref, pad_ref, sh_ref, hid_ref,
):
    strip_refs = (full_ref, before_ref, after_ref)
    fill_shifted(info_ref, x_ref, strip_refs, top_ref, right_ref, left_ref, pad_ref, sh_ref)
    depthwise(sh_ref, kern_ref, hid_ref)
    hidden = hid_ref[...].reshape(S * S, LANES)
    hidden_ref[0] = hidden
    _, _, normed = normalise(hidden, gain_ref[...])
    linear = mm(normed, w_in_ref[...])
    act = 0.5 * linear * (1.0 + jnp.tanh(ROOT * (linear + CUBE * linear * linear * linear)))
    mixed = mm(act.astype(BF), w_out_ref[...])
    current = (x_ref[0].reshape(S * S, LANES).astype(F32) + mixed).astype(BF)
    next_ref[0] = current.reshape(S, S, LANES)
    next_strips_ref[0] = mm(extract_ref[...], current).astype(BF).reshape(4, EDGE, LANES)


def backward_kernel(
    first, info_ref, x_ref, strip_refs, grad_ref, extra_ref, top_ref, right_ref, left_ref, place_ref, top_t_ref,
    right_t_ref, left_t_ref, kern_ref, gain_ref, w_in_ref, w_in_t_ref, w_out_t_ref,
    base_ref, canon_ref, kg_ref, gg_ref, wi_ref, wo_ref,
    pad_ref, sh_ref, hid_ref, gsh_ref, gh_ref, sum_ref, bl_ref, br_ref,
):
    @pl.when(pl.program_id(0) == 0)
    def _():
        kg_ref[...] = jnp.zeros_like(kg_ref)
        gg_ref[...] = jnp.zeros_like(gg_ref)
        wi_ref[...] = jnp.zeros_like(wi_ref)
        wo_ref[...] = jnp.zeros_like(wo_ref)
        gsh_ref[...] = jnp.zeros_like(gsh_ref)

    fill_shifted(info_ref, x_ref, strip_refs, top_ref, right_ref, left_ref, pad_ref, sh_ref)
    if first:
        depthwise(sh_ref, kern_ref, hid_ref)
        hidden = hid_ref[...].reshape(S * S, LANES)
        gradient = grad_ref[0].reshape(S * S, LANES).astype(F32)
    else:
        hidden = extra_ref[0][0]
        back = (extra_ref[1][...] + extra_ref[2][...].astype(F32)).astype(BF)
        gradient = grad_ref[0].reshape(S * S, LANES) + mm(
            place_ref[...], back.reshape(4 * EDGE, LANES)
        )
    sum_ref[...] = gradient.reshape(S, S, LANES)
    low = gradient.astype(BF)
    gain = gain_ref[...]
    standard, inverse, normed = normalise(hidden, gain)
    linear = mm(normed, w_in_ref[...])
    square = linear * linear
    tanh = jnp.tanh(ROOT * linear * (1.0 + CUBE * square))
    half = 0.5 * (1.0 + tanh)
    act = (linear * half).astype(BF)
    slope = half + linear * (0.5 * ROOT) * (1.0 - tanh * tanh) * (1.0 + (3.0 * CUBE) * square)
    grad_act = mm(low, w_out_t_ref[...])
    grad_linear = (slope * grad_act).astype(BF)
    over_pixels = (((0,), (0,)), ((), ()))
    wo_ref[...] += lax.dot_general(low, act, over_pixels, preferred_element_type=F32)
    wi_ref[...] += lax.dot_general(normed, grad_linear, over_pixels, preferred_element_type=F32)
    grad_normed = mm(grad_linear, w_in_t_ref[...])
    scaled = grad_normed * gain
    gg_ref[...] += jnp.sum((grad_normed * standard).reshape(S * S // 8, 8, LANES), 0)
    grad_hidden = inverse * (
        scaled
        - jnp.mean(scaled, -1, keepdims=True)
        - standard * jnp.mean(scaled * standard, -1, keepdims=True)
    )
    gh_ref[...] = grad_hidden.reshape(S, 2, 8, LANES)

    def column(b, carry):
        gh = gh_ref[...]
        for a in range(KS):
            kg_ref[b * KS + a] += jnp.sum(sh_ref[b, a : a + S] * gh, axis=(0, 1))
        taps = [kern_ref[b * KS + a][None] for a in range(KS)]
        for r in range(S + 2 * PAD):
            total = None
            for a in range(KS):
                if 0 <= r - a < S:
                    term = gh[r - a] * taps[a]
                    total = term if total is None else total + term
            gsh_ref[b, r, 16:32, :] = total.reshape(S, LANES)
        return carry

    lax.fori_loop(0, KS, column, 0)

    def rows(block, carry):
        row = block * 4
        total = gsh_ref[0, pl.ds(PAD + row, 4), 11:43, :]
        for b in range(1, KS):
            total = total + gsh_ref[b, pl.ds(PAD + row, 4), 11 - b : 43 - b, :]
        base_ref[0, pl.ds(row, 4)] = sum_ref[pl.ds(row, 4)] + total[:, 8:24]
        bl_ref[pl.ds(row, 4)] = total[:, 0:8]
        br_ref[pl.ds(row, 4)] = total[:, 24:32]
        return carry

    lax.fori_loop(0, S // 4, rows, 0)

    def outer(start):
        total = gsh_ref[0, start : start + PAD, 19:35, :]
        for b in range(1, KS):
            total = total + gsh_ref[b, start : start + PAD, 19 - b : 35 - b, :]
        return total.reshape(EDGE, LANES).astype(BF)

    canon_ref[0, 0] = mm(top_t_ref[...], outer(0)).astype(BF)
    canon_ref[0, 2] = outer(PAD + S)
    canon_ref[0, 1] = mm(right_t_ref[...], br_ref[...].reshape(S * 8, LANES).astype(BF)).astype(BF)
    canon_ref[0, 3] = mm(left_t_ref[...], bl_ref[...].reshape(S * 8, LANES).astype(BF)).astype(BF)


def whole(shape):
    return pl.BlockSpec(shape, lambda t, off: (0,) * len(shape))


def own_tile(shape, count):
    return pl.BlockSpec((1,) + shape, lambda t, off: (off[0] * count + t,) + (0,) * len(shape))


def each_tile(shape):
    return pl.BlockSpec((1,) + shape, lambda t, off: (t,) + (0,) * len(shape))


def shift_scratch():
    return [
        pltpu.VMEM((S + 2 * PAD, 32, LANES), F32),
        pltpu.VMEM((KS, S + 2 * PAD, 2, 8, LANES), F32),
        pltpu.VMEM((S, 2, 8, LANES), F32),
    ]


PARAMS = pltpu.CompilerParams(vmem_limit_bytes=58 * 1024 * 1024)


def forward_call(info, count, x, strips, tables, kern, gain, w_in, w_out):
    hidden_units = w_in.shape[1]
    return pl.pallas_call(
        forward_kernel,
        grid_spec=pltpu.PrefetchScalarGridSpec(
            num_scalar_prefetch=1,
            grid=(count,),
            in_specs=[
                own_tile((S, S, LANES), count),
                *[whole(part.shape) for part in strips],
                whole((EDGE, EDGE)),
                whole((S * 8, EDGE)),
                whole((S * 8, EDGE)),
                whole((4 * EDGE, S * S)),
                whole((KS * KS, 8, LANES)),
                whole((1, LANES)),
                whole((LANES, hidden_units)),
                whole((hidden_units, LANES)),
            ],
            out_specs=[
                each_tile((S * S, LANES)),
                each_tile((S, S, LANES)),
                each_tile((4, EDGE, LANES)),
            ],
            scratch_shapes=shift_scratch(),
        ),
        out_shape=[
            jax.ShapeDtypeStruct((count, S * S, LANES), F32),
            jax.ShapeDtypeStruct((count, S, S, LANES), BF),
            jax.ShapeDtypeStruct((count, 4, EDGE, LANES), BF),
        ],
        compiler_params=PARAMS,
        name="block_forward",
    )(info, x, *strips, *tables, kern, gain, w_in, w_out)


def first_backward(info_ref, x_ref, full_ref, before_ref, after_ref, grad_ref, *rest):
    backward_kernel(True, info_ref, x_ref, (full_ref, before_ref, after_ref), grad_ref, None, *rest)


def second_backward(
    info_ref, x_ref, full_ref, before_ref, after_ref, grad_ref, hidden_ref, own_ref, other_ref, *rest
):
    strip_refs = (full_ref, before_ref, after_ref)
    backward_kernel(False, info_ref, x_ref, strip_refs, grad_ref, (hidden_ref, own_ref, other_ref), *rest)


def collect_kernel(aims_ref, canon_ref, before_ref, after_ref, total_ref):
    total_ref[...] = jnp.zeros_like(total_ref)
    start = 0
    for source_ref in (canon_ref, before_ref, after_ref):

        def body(k, carry, source_ref=source_ref, start=start):
            aim = aims_ref[start + k]

            @pl.when(aim >= 0)
            def _():
                place = jnp.maximum(aim, 0)
                total_ref[place] = total_ref[place] + source_ref[k].astype(F32)

            return carry

        lax.fori_loop(0, source_ref.shape[0], body, 0)
        start += source_ref.shape[0]


def collect_call(aims, canon, before, after):
    rows = 2 * canon.shape[0]
    return pl.pallas_call(
        collect_kernel,
        grid_spec=pltpu.PrefetchScalarGridSpec(
            num_scalar_prefetch=1,
            grid=(1,),
            in_specs=[whole(canon.shape), whole(before.shape), whole(after.shape)],
            out_specs=whole((rows, EDGE, LANES)),
        ),
        out_shape=jax.ShapeDtypeStruct((rows, EDGE, LANES), F32),
        compiler_params=PARAMS,
        name="collect_strips",
    )(aims, canon, before, after)


def backward_call(first, info, count, x, strips, grad, extra, tables, kern, gain, w_in, w_in_t, w_out_t):
    hidden_units = w_in.shape[1]
    x_spec = each_tile((S, S, LANES)) if first else own_tile((S, S, LANES), count)
    grad_spec = own_tile((S, S, LANES), count) if first else each_tile((S, S, LANES))
    four = pl.BlockSpec((4, EDGE, LANES), lambda t, off: (t, 0, 0))
    extra_specs = [] if first else [each_tile((S * S, LANES)), four, four]
    return pl.pallas_call(
        first_backward if first else second_backward,
        grid_spec=pltpu.PrefetchScalarGridSpec(
            num_scalar_prefetch=1,
            grid=(count,),
            in_specs=[x_spec, *[whole(part.shape) for part in strips], grad_spec]
            + extra_specs
            + [whole(table.shape) for table in tables]
            + [
                whole((KS * KS, 8, LANES)),
                whole((1, LANES)),
                whole((LANES, hidden_units)),
                whole((hidden_units, LANES)),
                whole((LANES, hidden_units)),
            ],
            out_specs=[
                each_tile((S, S, LANES)),
                each_tile((4, EDGE, LANES)),
                whole((KS * KS, 8, LANES)),
                whole((8, LANES)),
                whole((LANES, hidden_units)),
                whole((LANES, hidden_units)),
            ],
            scratch_shapes=shift_scratch()
            + [
                pltpu.VMEM((KS, S + 2 * PAD, 48, LANES), F32),
                pltpu.VMEM((S, 2, 8, LANES), F32),
                pltpu.VMEM((S, S, LANES), F32),
                pltpu.VMEM((S, 8, LANES), F32),
                pltpu.VMEM((S, 8, LANES), F32),
            ],
        ),
        out_shape=[
            jax.ShapeDtypeStruct((count, S, S, LANES), F32),
            jax.ShapeDtypeStruct((count, 4, EDGE, LANES), BF),
            jax.ShapeDtypeStruct((KS * KS, 8, LANES), F32),
            jax.ShapeDtypeStruct((8, LANES), F32),
            jax.ShapeDtypeStruct((LANES, hidden_units), F32),
            jax.ShapeDtypeStruct((LANES, hidden_units), F32),
        ],
        compiler_params=PARAMS,
        name="block_backward",
    )(info, x, *strips, grad, *extra, *tables, kern, gain, w_in, w_in_t, w_out_t)


def shifted(value, axis, steps):
    count = lax.axis_size(axis)
    return lax.ppermute(value, axis, [(i, (i + steps) % count) for i in range(count)])


def swapped(value):
    return lax.ppermute(value, "chan", [(0, 1), (1, 0)])


def around(value):
    return shifted(value, "tile", 1), value, shifted(value, "tile", -1)


def ranked(mask):
    return jnp.cumsum(mask.astype(jnp.int32)) - 1


def picked(mask, values, first, width, empty):
    wanted = first + jnp.arange(width, dtype=jnp.int32)
    select = mask[None, :] & (ranked(mask)[None, :] == wanted[:, None])
    return jnp.max(jnp.where(select, values[None, :], empty), 1)


def in_rounds(rounds, body, state):
    return lax.while_loop(
        lambda carry: carry[0] < rounds,
        lambda carry: (carry[0] + 1, body(carry[0], carry[1])),
        (jnp.int32(1), state),
    )[1]


def highest(value, axis):
    count = lax.axis_size(axis)
    if count & (count - 1):
        return lax.pmax(value, axis)
    step = 1
    while step < count:
        value = jnp.maximum(value, lax.ppermute(value, axis, [(i, i ^ step) for i in range(count)]))
        step *= 2
    return value


def reduced(value, axis):
    count = lax.axis_size(axis)
    if count & (count - 1):
        return lax.psum(value.astype(BF), axis).astype(F32)
    step = 1
    while step < count:
        got = lax.ppermute(value.astype(BF), axis, [(i, i ^ step) for i in range(count)])
        value = value.astype(BF).astype(F32) + got.astype(F32)
        step *= 2
    return value


def local(activations, cotangent, neighbours, rotations, kernels, gains, w_in, w_out):
    tile_count = activations.shape[0]
    count = tile_count // 2
    chan = lax.axis_index("chan")
    position = lax.axis_index("tile")
    groups = lax.axis_size("tile")
    half_units = w_in.shape[2]

    extract, top, right, left = [jnp.asarray(table, BF) for table in permutation_tables()]
    forward_tables = (top, right, left, extract)
    backward_tables = (top, right, left, extract.T, top.T, right.T, left.T)

    seams = jnp.concatenate([neighbours, rotations], 1)
    side = jnp.arange(4, dtype=jnp.int32)

    def sides_of(block_seams):
        part = lax.dynamic_slice_in_dim(block_seams, chan * count, count, 0)
        source = (side[None, :] + 2 + part[:, 4:]) % 4
        owner = part[:, :4] // tile_count
        slot = (part[:, :4] % tile_count) * 4 + source
        return owner.reshape(-1), slot.reshape(-1)

    def mine_first(slot):
        return slot % (count * 4) + jnp.where(slot // (count * 4) == chan, 0, count * 4)

    seams_before, _, seams_after = around(seams)
    owner, slot = sides_of(seams)
    owner_before, slot_before = sides_of(seams_before)
    owner_after, slot_after = sides_of(seams_after)
    to_before = owner == (position - 1) % groups
    to_after = owner == (position + 1) % groups
    within = owner == position
    from_before = owner_before == position
    from_after = owner_after == position
    owners = (neighbours // tile_count).reshape(2, count * 4)
    before_count = jnp.sum((owners == (position - 1) % groups).astype(jnp.int32), 1)
    after_count = jnp.sum((owners == (position + 1) % groups).astype(jnp.int32), 1)
    most = jnp.broadcast_to(jnp.max(jnp.maximum(before_count, after_count)), (LANES,))
    rounds = (highest(most, "tile")[0] + count - 1) // count

    strips0 = jnp.einsum(
        "pk,tkc->tpc", extract, activations.reshape(tile_count, S * S, LANES), preferred_element_type=F32
    ).astype(BF).reshape(tile_count * 4, EDGE, LANES)

    def fetch(full, place):
        def ask(index):
            for_after = picked(from_after, place(slot_after), index * count, count, 0)
            for_before = picked(from_before, place(slot_before), index * count, count, 0)
            return (
                shifted(jnp.take(full, for_after, axis=0), "tile", 1),
                shifted(jnp.take(full, for_before, axis=0), "tile", -1),
            )

        def widened(got):
            return jnp.pad(got, ((0, 3 * count), (0, 0), (0, 0)))

        def more(index, state):
            return tuple(
                lax.dynamic_update_slice_in_dim(held, got, index * count, 0)
                for held, got in zip(state, ask(index))
            )

        before, after = in_rounds(rounds, more, tuple(widened(got) for got in ask(0)))
        base = full.shape[0]
        where_before = base + ranked(to_before)
        where_after = base + 4 * count + ranked(to_after)
        index = jnp.where(within, place(slot), jnp.where(to_before, where_before, where_after))
        return jnp.concatenate([chan.astype(jnp.int32).reshape(1), index]), (full, before, after)

    aim_within = jnp.where(within, mine_first(slot), -1)

    def returned(canon):
        canon = canon.reshape(count * 4, EDGE, LANES)
        numbers = jnp.arange(count * 4, dtype=jnp.int32)

        def send(index):
            for_before = picked(to_before, numbers, index * count, count, 0)
            for_after = picked(to_after, numbers, index * count, count, 0)
            aim_before = picked(from_before, mine_first(slot_before), index * count, count, -1)
            aim_after = picked(from_after, mine_first(slot_after), index * count, count, -1)
            got_before = shifted(jnp.take(canon, for_after, axis=0), "tile", 1)
            got_after = shifted(jnp.take(canon, for_before, axis=0), "tile", -1)
            return jnp.concatenate([aim_before, aim_after]), got_before, got_after

        aims, got_before, got_after = send(0)
        total = collect_call(jnp.concatenate([aim_within, aims]), canon, got_before, got_after)

        def more(index, total):
            aims, *got = send(index)
            aims = jnp.where(aims < 0, tile_count * 4, aims)
            return total.at[aims].add(jnp.concatenate(got, 0).astype(F32), mode="drop")

        total = in_rounds(rounds, more, total)
        return total, swapped(total[count * 4 :].astype(BF))

    joined = jnp.stack([w_in[0].T, w_in[1].T, w_out[0], w_out[1]], 0)
    gathered = lax.all_gather(joined, "chan", axis=1, tiled=True)
    in_t = [gathered[0], gathered[1]]
    out_w = [gathered[2], gathered[3]]
    in_w = [value.T for value in in_t]
    out_t = [value.T for value in out_w]
    taps = jnp.broadcast_to(
        kernels.astype(F32).transpose(0, 2, 1, 3).reshape(2, KS * KS, 1, LANES), (2, KS * KS, 8, LANES)
    )

    info0, chosen0 = fetch(strips0, lambda value: value)
    hidden0, current, strips1 = forward_call(
        info0, count, activations, chosen0, forward_tables, taps[0], gains[0:1], in_w[0], out_w[0]
    )
    strips1 = strips1.reshape(count * 4, EDGE, LANES)
    info1, chosen1 = fetch(jnp.concatenate([strips1, swapped(strips1)], 0), mine_first)
    base1, canon1, *grads1 = backward_call(
        True, info1, count, current, chosen1, cotangent, (), backward_tables,
        taps[1], gains[1:2], in_w[1], in_t[1], out_t[1],
    )

    def split(parts):
        kernel_part, gain_part, in_part, out_part = parts
        small = jnp.concatenate(
            [
                kernel_part.sum(1),
                gain_part.sum(0, keepdims=True),
            ],
            0,
        )
        stacked = jnp.stack([in_part, out_part], 0)

        def half(which):
            piece = lax.dynamic_slice_in_dim(stacked, which * half_units, half_units, 2)
            return jnp.concatenate([piece.reshape(-1, LANES), small], 0)

        total = half(chan) + swapped(half(1 - chan).astype(BF)).astype(F32)
        total = reduced(total, "tile")
        size = LANES * half_units // LANES
        kernel_sum = total[2 * size : 2 * size + KS * KS].reshape(KS, KS, LANES).transpose(1, 0, 2)
        return (
            kernel_sum,
            total[2 * size + KS * KS],
            total[:size].reshape(LANES, half_units),
            total[size : 2 * size].reshape(LANES, half_units).T,
        )

    sums1 = split(grads1)
    returned1 = returned(canon1)
    base0, canon0, *grads0 = backward_call(
        False, info0, count, activations, chosen0, base1, (hidden0, *returned1), backward_tables,
        taps[0], gains[0:1], in_w[0], in_t[0], out_t[0],
    )
    own0, other0 = returned(canon0)
    returned0 = (own0[: count * 4] + other0.astype(F32)).astype(BF)
    sums0 = split(grads0)
    placed = jnp.einsum(
        "kp,tpc->tkc", extract.T, returned0.reshape(count, 4 * EDGE, LANES), preferred_element_type=F32
    )
    own_out = (base0 + placed.reshape(base0.shape)).astype(BF)
    input_grads = lax.all_gather(own_out, "chan", axis=0, tiled=True)
    stacked = [jnp.stack([a, b], 0) for a, b in zip(sums0, sums1)]
    return (input_grads, *stacked)


def solution(mesh):
    placed = (
        P(("parts", "tile"), None, None, None),
        P(("parts", "tile"), None, None, None),
        P("tile", None),
        P("tile", None),
        P(),
        P(),
        P(None, None, "chan"),
        P(None, "chan", None),
    )
    return jax.shard_map(
        local,
        mesh=mesh,
        in_specs=placed,
        out_specs=(
            P(("parts", "tile"), None, None, None),
            P("parts", None, None, None),
            P("parts", None),
            P("parts", None, "chan"),
            P("parts", "chan", None),
        ),
        check_vma=False,
    )
```
